32 devices in a mesh: dp: 8 (over z, y), tensor: 4 (over x, core).
Axes of the slice: x: 2, y: 2, z: 4, core: 2. Of those that a mesh axis runs over, the one named last changes fastest.
Arguments:
- tokens: bfloat16 [1024, 2048], P('dp', 'tensor'), may hold values from -6 to 6
- cotangent: bfloat16 [1024, 2048], P('dp', 'tensor'), may hold values from -6 to 6
- pair_ids: int32 [1024], P('dp'), may hold values from 0 to 99, as said below
- up_mask: int32 [100, 16, 64], P(None, None, 'tensor'), may hold values 0 or 1
- down_mask: int32 [100, 64, 16], P(None, 'tensor'), may hold values 0 or 1
- up_weight: bfloat16 [2048, 8192], P(None, 'tensor'), may hold values from -0.125 to 0.125
- down_weight: bfloat16 [8, 8192, 2048], P('dp', 'tensor'), may hold values from -0.0625 to 0.0625
Outputs:
- mixed: bfloat16 [1024, 2048], P('dp', 'tensor')
- token_grads: bfloat16 [1024, 2048], P('dp', 'tensor')
The draws below stay inside these ranges and needn't reach their ends.
Inputs may be any that keep to these rules, and one draw needn't show every extreme that they name: `pair_ids`: within each aligned block of 128 tokens (the tokens of one index of dp) at most 24 tokens belong to one language group; in every draw 1 group hold exactly 24 tokens of every block.
All inputs are finite; a program needn't handle non-finite values. No bound on the sum of `up_mask` or of `down_mask` on one device may be relied on, other than what follows from the above.
Results may differ from the reference program's by a relative error of at most 0.014.
Values may be sent and summed in bfloat16 or wider, within the bound.
A program may use at most 128 MiB of HBM per device.

```python
import jax
import jax.numpy as jnp
from jax import lax

D = 2048
FF = 8192
BLOCK = 128
PAIRS = 100
TOK_DEV = 128
OWNERS = 8
CAP = 24
HOT = 1
TOKENS = 1024
N_TENSOR = 4


def draw_pair_ids(key, part):
    slot_entries = OWNERS * CAP
    key_hot, key_score, key_choose, key_order = jax.random.split(key, 4)
    hottest = jax.random.permutation(key_hot, OWNERS)[:HOT]
    frequent_flag = jnp.any(jnp.arange(OWNERS)[:, None] == hottest[None, :], axis=1)
    slot_group_index = jnp.arange(slot_entries) // CAP
    extra_score = jnp.where(frequent_flag[slot_group_index], 1 << 29, 0).astype(jnp.int32)
    noise_portion = jax.random.randint(key_score, (OWNERS, slot_entries), 0, 1 << 18)
    ranking_values = noise_portion * slot_entries + jnp.arange(slot_entries, dtype=jnp.int32)[None, :] + extra_score[None, :]
    chosen = lax.top_k(ranking_values, TOK_DEV)[1]
    groups = chosen // CAP
    choices_here = (PAIRS - 1 - groups) // OWNERS + 1
    offsets = jax.random.randint(key_choose, groups.shape, 0, choices_here)
    pairs = groups + OWNERS * offsets
    order_keys = jax.random.split(key_order, OWNERS)
    pairs = jax.vmap(jax.random.permutation)(order_keys, pairs)
    return pairs.reshape(-1).astype(jnp.int32)


def touch_ends(values, key, smallest, largest):
    shape = values.shape
    index_at = [jax.random.randint(jax.random.fold_in(key, axis), (), 0, shape[axis]) for axis in range(len(shape))]
    values = values.at[tuple(index_at)].set(smallest)
    longest = shape.index(max(shape))
    index_at[longest] = (index_at[longest] + 1) % shape[longest]
    return values.at[tuple(index_at)].set(largest)


def block_scale(own_key, shape, shards, smallest, largest):
    loudness, own = 1.0, jax.random.fold_in(own_key, 6)
    for dim, parts in shards:
        draws = jnp.exp(jax.random.uniform(jax.random.fold_in(own, dim), (parts,), jnp.float32, smallest / len(shards), largest / len(shards)))
        loudness = loudness * jnp.repeat(draws, shape[dim] // parts).reshape([-1 if axis == dim else 1 for axis in range(len(shape))])
    return loudness


def bell_draw(rng, extent, scale, bound, pieces=(), kind=jnp.bfloat16):
    drawn = scale * jax.random.normal(rng, extent, jnp.float32)
    if pieces:
        drawn = drawn * block_scale(rng, extent, pieces, -0.22, 0.18)
    return jnp.clip(drawn, -bound, bound).astype(kind)


def setup_inputs(seed: int = 0) -> dict:
    seeds = jax.random.split(jax.random.key(seed), 8)
    tokens = bell_draw(seeds[0], (TOKENS, D), 1.0, 6.0, ((0, 8), (1, 4)))
    cotangent = bell_draw(seeds[1], (TOKENS, D), 1.0, 6.0, ((0, 8), (1, 4)))
    pair_ids = draw_pair_ids(jax.random.fold_in(seeds[7], 71), 0)
    up_mask = touch_ends((jax.random.randint(seeds[3], (PAIRS, D // BLOCK, FF // BLOCK), 0, 4) < 3).astype(jnp.int32), jax.random.fold_in(seeds[3], 1), 0, 1)
    down_mask = touch_ends((jax.random.randint(seeds[4], (PAIRS, FF // BLOCK, D // BLOCK), 0, 4) < 3).astype(jnp.int32), jax.random.fold_in(seeds[4], 1), 0, 1)
    up_weight = bell_draw(seeds[5], (D, FF), D ** -0.5, 0.125, ((1, 4),))
    down_weight = bell_draw(seeds[6], (OWNERS, FF, D), FF ** -0.5, 0.0625, ((0, 8), (1, 4)))
    return {"tokens": tokens, "cotangent": cotangent, "pair_ids": pair_ids, "up_mask": up_mask, "down_mask": down_mask, "up_weight": up_weight, "down_weight": down_weight}


highest = lax.Precision.HIGHEST

def product_plain(inputs, weight, masks):
    columns = weight.shape[1]
    blocks_out = columns // BLOCK
    spread = jnp.repeat(jnp.transpose(masks, (2, 0, 1)), BLOCK, axis=2)
    masked = inputs.astype(jnp.float32)[None, :, :] * spread
    weight_tiles = weight.astype(jnp.float32).reshape(weight.shape[0], blocks_out, BLOCK)
    result = jnp.einsum('nrk,knc->rnc', masked, weight_tiles, precision=highest)
    return result.reshape(inputs.shape[0], columns)

def product_turned(inputs, weight, masks):
    columns = weight.shape[0]
    blocks_out = columns // BLOCK
    spread = jnp.repeat(jnp.transpose(masks, (1, 0, 2)), BLOCK, axis=2)
    masked = inputs.astype(jnp.float32)[None, :, :] * spread
    weight_tiles = weight.astype(jnp.float32).reshape(blocks_out, BLOCK, weight.shape[1])
    result = jnp.einsum('nrk,nck->rnc', masked, weight_tiles, precision=highest)
    return result.reshape(inputs.shape[0], columns)

def mask_rows(mask_table, pairs_here):
    safe_pairs = jnp.maximum(pairs_here, 0)
    looked = mask_table[safe_pairs].astype(jnp.float32)
    return jnp.where((pairs_here >= 0)[:, None, None], looked, jnp.zeros_like(looked))

def slot_table(pair_ids):
    target = (pair_ids % OWNERS).reshape(OWNERS, TOK_DEV)
    matches = (target[:, :, None] == jnp.arange(OWNERS, dtype=jnp.int32)[None, None, :]).astype(jnp.int32)
    before = lax.optimization_barrier(jnp.sum((jnp.cumsum(matches, axis=1) - matches) * matches, axis=2))
    source = jnp.arange(OWNERS, dtype=jnp.int32)[:, None]
    position = ((target * OWNERS + source) * CAP + before).astype(jnp.int32)
    token_index = jnp.arange(TOKENS, dtype=jnp.int32)
    filled = jnp.full((OWNERS * OWNERS * CAP,), TOKENS, jnp.int32).at[position.reshape(-1)].set(token_index)
    return filled.reshape(OWNERS, OWNERS * CAP)

def shard_sums_down(hidden, down_group, down_rows):
    width = FF // N_TENSOR
    blocks = width // BLOCK
    total = jnp.zeros((hidden.shape[0], D), jnp.float32)
    for shard in range(N_TENSOR):
        part = product_plain(hidden[:, shard * width:(shard + 1) * width], down_group[shard * width:(shard + 1) * width, :], down_rows[:, shard * blocks:(shard + 1) * blocks, :])
        rounded = lax.optimization_barrier(part.astype(jnp.bfloat16))
        total = total + rounded.astype(jnp.float32)
    return total.astype(jnp.bfloat16)

def shard_sums_up(grad_pre, up_weight, up_rows):
    width = FF // N_TENSOR
    blocks = width // BLOCK
    total = jnp.zeros((grad_pre.shape[0], D), jnp.float32)
    for shard in range(N_TENSOR):
        part = product_turned(grad_pre[:, shard * width:(shard + 1) * width], up_weight[:, shard * width:(shard + 1) * width], up_rows[:, :, shard * blocks:(shard + 1) * blocks])
        rounded = lax.optimization_barrier(part.astype(jnp.bfloat16))
        total = total + rounded.astype(jnp.float32)
    return total.astype(jnp.bfloat16)

def reference(tokens, cotangent, pair_ids, up_mask, down_mask, up_weight, down_weight):
    pair_table = slot_table(pair_ids)
    padded_tokens = jnp.concatenate([tokens, jnp.zeros((1, D), tokens.dtype)], axis=0)
    padded_grads = jnp.concatenate([cotangent, jnp.zeros((1, D), cotangent.dtype)], axis=0)
    padded_pairs = jnp.concatenate([pair_ids, jnp.full((1,), -1, jnp.int32)]).astype(jnp.int32)

    def one_group(packed):
        indices, down_group = packed
        pairs_here = padded_pairs[indices]
        up_rows = mask_rows(up_mask, pairs_here)
        down_rows = mask_rows(down_mask, pairs_here)
        before_act = product_plain(padded_tokens[indices], up_weight, up_rows)
        activated, backward_function = jax.vjp(jax.nn.gelu, before_act)
        hidden = activated.astype(jnp.bfloat16)
        mixed_rows = shard_sums_down(hidden, down_group, down_rows)
        grad_hidden = product_turned(padded_grads[indices], down_group, down_rows)
        grad_pre = backward_function(grad_hidden)[0].astype(jnp.bfloat16)
        input_rows = shard_sums_up(grad_pre, up_weight, up_rows)
        return (mixed_rows, input_rows)
    mixed_all, grads_all = lax.map(one_group, (pair_table, down_weight))
    flat_index = pair_table.reshape(-1)
    mixed = jnp.zeros((TOKENS + 1, D), jnp.bfloat16).at[flat_index].set(mixed_all.reshape(-1, D))[:TOKENS]
    token_grads = jnp.zeros((TOKENS + 1, D), jnp.bfloat16).at[flat_index].set(grads_all.reshape(-1, D))[:TOKENS]
    return (mixed, token_grads)
```

```python
import functools

import jax
import jax.numpy as jnp
from jax import lax
from jax.experimental import pallas as pl
from jax.experimental.pallas import tpu as pltpu
from jax.sharding import PartitionSpec as P

BLOCK = 128
ROOT = 0.7978845608028654
CUBE = 0.044715
NT = (((1,), (1,)), ((), ()))
NN = (((1,), (0,)), ((), ()))


def dot(a, b, dims=NN):
    return lax.dot_general(a, b, dims, preferred_element_type=jnp.float32)


def gelu_pair(v):
    square = v * v
    t = jnp.tanh(ROOT * (v + CUBE * v * square))
    half = 0.5 * (1.0 + t)
    slope = half + 0.5 * v * (1.0 - t * t) * (ROOT * (1.0 + 3.0 * CUBE * square))
    return v * half, slope


def masked(values_ref, bits, blocks):
    rows = values_ref.shape[0]
    parts = []
    for b in range(blocks):
        own = jnp.broadcast_to(bits[:, b : b + 1], (rows, BLOCK))
        parts.append(values_ref[:, b * BLOCK : (b + 1) * BLOCK] * own)
    return jnp.concatenate(parts, axis=1)


def products(x_ref, g_ref, pick, up_ref, down_ref, wu_ref, wd_ref, h_ref, q_ref, mixed_ref, input_ref):
    blocks_d, blocks_f = up_ref.shape[0], up_ref.shape[1]

    def first(f, _):
        at = pl.ds(pl.multiple_of(f * BLOCK, BLOCK), BLOCK)
        up_bits = dot(pick, up_ref[:, f, :].astype(jnp.bfloat16), NT).astype(jnp.bfloat16)
        down_bits = dot(pick, down_ref[f].astype(jnp.bfloat16), NT).astype(jnp.bfloat16)
        pre = dot(masked(x_ref, up_bits, blocks_d), wu_ref[:, at])
        grad = dot(masked(g_ref, down_bits, blocks_d), wd_ref[at, :], NT)
        act, slope = gelu_pair(pre)
        h_ref[:, at] = act.astype(jnp.bfloat16)
        q_ref[:, at] = (grad * slope).astype(jnp.bfloat16)
        return 0

    def second(d, _):
        at = pl.ds(pl.multiple_of(d * BLOCK, BLOCK), BLOCK)
        up_bits = dot(pick, up_ref[d].astype(jnp.bfloat16), NT).astype(jnp.bfloat16)
        down_bits = dot(pick, down_ref[:, d, :].astype(jnp.bfloat16), NT).astype(jnp.bfloat16)
        mixed_ref[:, at] = dot(masked(h_ref, down_bits, blocks_f), wd_ref[:, at]).astype(jnp.bfloat16)
        input_ref[:, at] = dot(masked(q_ref, up_bits, blocks_f), wu_ref[at, :], NT).astype(jnp.bfloat16)
        return 0

    lax.fori_loop(0, blocks_f, first, 0)
    lax.fori_loop(0, blocks_d, second, 0)


def compute_kernel(x_ref, g_ref, pick_ref, up_ref, down_ref, wu_hbm, wd_hbm, mixed_ref, input_ref,
                   wu_ref, wd_ref, h_ref, q_ref, sems):
    load_up = pltpu.make_async_copy(wu_hbm, wu_ref, sems.at[0])
    load_down = pltpu.make_async_copy(wd_hbm, wd_ref, sems.at[1])
    load_up.start()
    load_down.start()
    load_up.wait()
    load_down.wait()
    products(x_ref, g_ref, pick_ref[...], up_ref, down_ref, wu_ref, wd_ref, h_ref, q_ref, mixed_ref, input_ref)


def compute(x, g, pick, up_table, down_table, up_weight, down_weight):
    rows, width = x.shape
    hidden = up_weight.shape[1]
    vmem = pl.BlockSpec(memory_space=pltpu.VMEM)
    anywhere = pl.BlockSpec(memory_space=pl.ANY)
    return pl.pallas_call(
        compute_kernel,
        out_shape=[jax.ShapeDtypeStruct((rows, width), jnp.bfloat16)] * 2,
        in_specs=[vmem] * 5 + [anywhere] * 2,
        out_specs=[vmem] * 2,
        scratch_shapes=[
            pltpu.VMEM(up_weight.shape, jnp.bfloat16),
            pltpu.VMEM(down_weight.shape, jnp.bfloat16),
            pltpu.VMEM((rows, hidden), jnp.bfloat16),
            pltpu.VMEM((rows, hidden), jnp.bfloat16),
            pltpu.SemaphoreType.DMA((2,)),
        ],
        compiler_params=pltpu.CompilerParams(vmem_limit_bytes=44 * 2**20),
        name="masked_products",
    )(x, g, pick, up_table, down_table, up_weight, down_weight)


def place(pair_ids, groups, capacity):
    target = pair_ids % groups
    matches = (target[:, None] == jnp.arange(groups, dtype=jnp.int32)[None, :]).astype(jnp.int32)
    before = jnp.sum((jnp.cumsum(matches, axis=0) - matches) * matches, axis=1)
    position = target * capacity + before
    slots = jnp.arange(groups * capacity, dtype=jnp.int32)
    return (position[None, :] == slots[:, None]).astype(jnp.bfloat16)


def swap(values, groups, capacity):
    width = values.shape[1]
    moved = lax.all_to_all(
        values.reshape(groups, capacity, width), "dp", split_axis=0, concat_axis=0, tiled=True
    )
    return moved.reshape(groups * capacity, width)


def per_device(tokens, cotangent, pair_ids, up_mask, down_mask, up_weight, down_weight):
    groups = lax.axis_size("dp")
    tok_count, part = tokens.shape
    pairs = up_mask.shape[0]
    capacity = max(2, (3 * tok_count + 2 * groups - 1) // (2 * groups))
    slot_count = groups * capacity
    placer = place(pair_ids, groups, capacity)
    lanes = -(-pairs // BLOCK) * BLOCK
    known = (pair_ids[:, None] == jnp.arange(lanes, dtype=jnp.int32)[None, :]).astype(jnp.bfloat16)
    pad = ((0, 0), (0, 0), (0, lanes - pairs))
    up_table = jnp.pad(jnp.transpose(up_mask, (1, 2, 0)), pad)
    down_table = jnp.pad(jnp.transpose(down_mask, (1, 2, 0)), pad)

    leaving = jnp.concatenate([tokens, cotangent, known], axis=1)
    moved = swap(dot(placer, leaving).astype(jnp.bfloat16), groups, capacity)
    both = jnp.stack([moved[:, :part], moved[:, part : 2 * part]])
    whole = lax.all_gather(both, "tensor", axis=2, tiled=True)
    mixed_part, input_part = compute(
        whole[0], whole[1], moved[:, 2 * part :], up_table, down_table, up_weight, down_weight[0]
    )
    summed = lax.psum_scatter(
        jnp.stack([mixed_part, input_part]), "tensor", scatter_dimension=2, tiled=True
    )
    back = swap(jnp.concatenate([summed[0], summed[1]], axis=1), groups, capacity)
    out = lax.dot_general(
        placer, back, (((0,), (0,)), ((), ())), preferred_element_type=jnp.float32
    ).astype(jnp.bfloat16)
    return out[:, :part], out[:, part:]


def solution(mesh):
    return jax.shard_map(
        per_device,
        mesh=mesh,
        in_specs=(
            P("dp", "tensor"),
            P("dp", "tensor"),
            P("dp"),
            P(None, None, "tensor"),
            P(None, "tensor", None),
            P(None, "tensor"),
            P("dp", "tensor", None),
        ),
        out_specs=(P("dp", "tensor"), P("dp", "tensor")),
        check_vma=False,
    )
```

```python
import functools

import jax
import jax.numpy as jnp
from jax import lax
from jax.experimental import pallas as pl
from jax.experimental.pallas import tpu as pltpu
from jax.sharding import PartitionSpec as P

BLOCK = 128
ROOT = 0.7978845608028654
CUBE = 0.044715
NT = (((1,), (1,)), ((), ()))
NN = (((1,), (0,)), ((), ()))


def dot(a, b, dims=NN):
    return lax.dot_general(a, b, dims, preferred_element_type=jnp.float32)


def gelu_pair(v):
    square = v * v
    t = jnp.tanh(ROOT * (v + CUBE * v * square))
    half = 0.5 * (1.0 + t)
    slope = half + 0.5 * v * (1.0 - t * t) * (ROOT * (1.0 + 3.0 * CUBE * square))
    return v * half, slope


def masked(values_ref, bits, blocks):
    rows = values_ref.shape[0]
    parts = []
    for b in range(blocks):
        own = jnp.broadcast_to(bits[:, b : b + 1], (rows, BLOCK))
        parts.append(values_ref[:, b * BLOCK : (b + 1) * BLOCK] * own)
    return jnp.concatenate(parts, axis=1)


def products(x_ref, g_ref, pick, up_ref, down_ref, wu_ref, wd_ref, h_ref, q_ref, mixed_ref, input_ref):
    blocks_d, blocks_f = up_ref.shape[0], up_ref.shape[1]

    def first(f, _):
        at = pl.ds(pl.multiple_of(f * BLOCK, BLOCK), BLOCK)
        up_bits = dot(pick, up_ref[:, f, :].astype(jnp.bfloat16), NT).astype(jnp.bfloat16)
        down_bits = dot(pick, down_ref[f].astype(jnp.bfloat16), NT).astype(jnp.bfloat16)
        pre = dot(masked(x_ref, up_bits, blocks_d), wu_ref[:, at])
        grad = dot(masked(g_ref, down_bits, blocks_d), wd_ref[at, :], NT)
        act, slope = gelu_pair(pre)
        h_ref[:, at] = act.astype(jnp.bfloat16)
        q_ref[:, at] = (grad * slope).astype(jnp.bfloat16)
        return 0

    def second(d, _):
        at = pl.ds(pl.multiple_of(d * BLOCK, BLOCK), BLOCK)
        up_bits = dot(pick, up_ref[d].astype(jnp.bfloat16), NT).astype(jnp.bfloat16)
        down_bits = dot(pick, down_ref[:, d, :].astype(jnp.bfloat16), NT).astype(jnp.bfloat16)
        mixed_ref[:, at] = dot(masked(h_ref, down_bits, blocks_f), wd_ref[:, at]).astype(jnp.bfloat16)
        input_ref[:, at] = dot(masked(q_ref, up_bits, blocks_f), wu_ref[at, :], NT).astype(jnp.bfloat16)
        return 0

    lax.fori_loop(0, blocks_f, first, 0)
    lax.fori_loop(0, blocks_d, second, 0)


def compute_kernel(x_ref, g_ref, pick_ref, up_ref, down_ref, wu_hbm, wd_hbm, mixed_ref, input_ref,
                   wu_ref, wd_ref, h_ref, q_ref, sems):
    load_up = pltpu.make_async_copy(wu_hbm, wu_ref, sems.at[0])
    load_down = pltpu.make_async_copy(wd_hbm, wd_ref, sems.at[1])
    load_up.start()
    load_down.start()
    load_up.wait()
    load_down.wait()
    products(x_ref, g_ref, pick_ref[...], up_ref, down_ref, wu_ref, wd_ref, h_ref, q_ref, mixed_ref, input_ref)


def compute(x, g, pick, up_table, down_table, up_weight, down_weight):
    rows, width = x.shape
    hidden = up_weight.shape[1]
    vmem = pl.BlockSpec(memory_space=pltpu.VMEM)
    anywhere = pl.BlockSpec(memory_space=pl.ANY)
    return pl.pallas_call(
        compute_kernel,
        out_shape=[jax.ShapeDtypeStruct((rows, width), jnp.bfloat16)] * 2,
        in_specs=[vmem] * 5 + [anywhere] * 2,
        out_specs=[vmem] * 2,
        scratch_shapes=[
            pltpu.VMEM(up_weight.shape, jnp.bfloat16),
            pltpu.VMEM(down_weight.shape, jnp.bfloat16),
            pltpu.VMEM((rows, hidden), jnp.bfloat16),
            pltpu.VMEM((rows, hidden), jnp.bfloat16),
            pltpu.SemaphoreType.DMA((2,)),
        ],
        compiler_params=pltpu.CompilerParams(vmem_limit_bytes=44 * 2**20),
        name="masked_products",
    )(x, g, pick, up_table, down_table, up_weight, down_weight)


MESH = pl.DeviceIdType.MESH


def stacked(values, row, count):
    wide = values.shape[1] // BLOCK
    return jnp.concatenate(
        [values[row : row + count, b * BLOCK : (b + 1) * BLOCK] for b in range(wide)], axis=0
    ).astype(jnp.bfloat16)


def unstack(slab, into_ref, row, column, count):
    wide = slab.astype(jnp.float32)
    for b in range(slab.shape[0] // count):
        into_ref[row : row + count, column + b * BLOCK : column + (b + 1) * BLOCK] = wide[
            b * count : (b + 1) * count
        ]


def layer_kernel(groups, capacity, tokens_ref, cotangent_ref, pairs_ref, up_ref, down_ref, wu_hbm, wd_hbm,
                 mixed_ref, grads_ref,
                 wu_ref, wd_ref, eu_ref, ed_ref, send_p, send_a, send_b, got_p, got_a, got_b,
                 wide_ref, x_ref, g_ref, h_ref, q_ref, slope_ref,
                 part_m, part_i, sib_m, sib_i, out_m, out_i, in_m, in_i,
                 back_m, back_i, home_m, home_i, local_sems, ss, rs):
    slots = groups * capacity
    blocks_d, blocks_f = up_ref.shape[0], up_ref.shape[1]
    tok_count, part = tokens_ref.shape
    blocks_p = part // BLOCK
    lanes = up_ref.shape[2]
    me, t = lax.axis_index("dp"), lax.axis_index("tensor")
    core, x = t % 2, t // 2
    sibling, across = 2 * x + 1 - core, 2 * (1 - x) + core
    others = [(me + k) % groups for k in range(1, groups)]

    load_up = pltpu.make_async_copy(wu_hbm, wu_ref, local_sems.at[0])
    load_down = pltpu.make_async_copy(wd_hbm, wd_ref, local_sems.at[1])
    load_up.start()
    load_down.start()

    barrier = pltpu.get_barrier_semaphore()
    for j in others:
        pl.semaphore_signal(barrier, inc=1, device_id={"dp": j}, device_id_type=MESH)
    for s in (sibling, across):
        pl.semaphore_signal(barrier, inc=1, device_id={"tensor": s}, device_id_type=MESH)

    pairs = pairs_ref[...]
    target = lax.rem(pairs, jnp.full_like(pairs, groups))
    group_of = lax.broadcasted_iota(jnp.int32, (groups, tok_count), 0)
    match = group_of == target
    earlier = (
        lax.broadcasted_iota(jnp.int32, (tok_count, tok_count), 0)
        < lax.broadcasted_iota(jnp.int32, (tok_count, tok_count), 1)
    ).astype(jnp.float32).astype(jnp.bfloat16)
    before = dot(match.astype(jnp.float32).astype(jnp.bfloat16), earlier)
    spot = before + (group_of * capacity).astype(jnp.float32)
    position = jnp.sum(jnp.where(match, spot, 0.0), axis=0, keepdims=True)
    slot_of = lax.broadcasted_iota(jnp.int32, (slots, tok_count), 0).astype(jnp.float32)
    placed = (slot_of == position).astype(jnp.float32)
    placer = placed.astype(jnp.bfloat16)
    placer_turned = placed.T.astype(jnp.bfloat16)
    known = (lax.broadcasted_iota(jnp.int32, (lanes, tok_count), 0) == pairs).astype(jnp.float32)
    moved = dot(placer, known.astype(jnp.bfloat16), NT)
    room = send_p.shape[1] - capacity
    for j in range(groups):
        own = moved[j * capacity : (j + 1) * capacity]
        if room:
            own = jnp.concatenate([own, jnp.zeros((room, lanes), jnp.float32)], axis=0)
        send_p[j] = own.astype(jnp.bfloat16)
    got_p[me] = send_p[me]

    pl.semaphore_wait(barrier, groups + 1)

    def remote(src, dst, sem, where):
        return pltpu.make_async_remote_copy(
            src_ref=src, dst_ref=dst, send_sem=ss.at[sem], recv_sem=rs.at[sem],
            device_id=where, device_id_type=MESH,
        )

    step = groups - 1
    every = []

    def launch(copies):
        for copy in copies:
            copy.start()
        every.extend(copies)
        return copies

    def arrive(copies):
        for copy in copies:
            copy.wait_recv()

    trip_p = launch([
        remote(send_p.at[j], got_p.at[me], k, {"dp": j}) for k, j in enumerate(others)
    ])

    def dispatch(values_ref, send, got, first):
        moved = dot(placer, values_ref[...])
        for j in range(groups):
            send[j] = stacked(moved, j * capacity, capacity)
        got[t, me] = send[me]
        return launch([
            remote(send.at[j], got.at[t, me], first + k, {"dp": j}) for k, j in enumerate(others)
        ])

    trip_a = dispatch(tokens_ref, send_a, got_a, step)
    trip_b = dispatch(cotangent_ref, send_b, got_b, 2 * step)
    base = 3 * step

    def share(got, first):
        return launch([
            remote(got.at[t], got.at[t], first, {"tensor": across}),
            remote(got.at[t], got.at[t], first + 1, {"tensor": sibling}),
        ])

    def forward(got, first):
        return launch([remote(got.at[across], got.at[across], first + 2, {"tensor": sibling})])

    arrive(trip_p)
    for i in range(groups):
        unstack(got_p[i, :capacity], wide_ref, i * capacity, 0, capacity)
    pick = wide_ref[:, :lanes].astype(jnp.bfloat16)

    def expand(table, into_ref, f):
        bits = dot(pick, table.astype(jnp.float32).astype(jnp.bfloat16), NT).astype(jnp.bfloat16)
        for d in range(blocks_d):
            into_ref[f, :, d * BLOCK : (d + 1) * BLOCK] = jnp.broadcast_to(
                bits[:, d : d + 1], (slots, BLOCK)
            )

    def expand_up(f, _):
        expand(up_ref[:, f, :], eu_ref, f)
        return 0

    def expand_down(f, _):
        expand(down_ref[f], ed_ref, f)
        return 0

    lax.fori_loop(0, blocks_f, expand_up, 0)
    arrive(trip_a)
    share_a = share(got_a, base)
    half = blocks_f // 2
    lax.fori_loop(0, half, expand_down, 0)
    arrive(share_a[:1])
    forward_a = forward(got_a, base)
    lax.fori_loop(half, blocks_f, expand_down, 0)
    arrive(trip_b)
    share_b = share(got_b, base + 3)
    arrive(share_a[1:] + forward_a)

    def assemble(got, into_ref):
        for s in range(got.shape[0]):
            for i in range(groups):
                unstack(got[s, i], wide_ref, i * capacity, s * part, capacity)
        into_ref[...] = wide_ref[...].astype(jnp.bfloat16)

    assemble(got_a, x_ref)
    load_up.wait()

    def columns(b):
        return pl.ds(pl.multiple_of(b * BLOCK, BLOCK), BLOCK)

    def pre_step(f, _):
        pre = dot(x_ref[...] * eu_ref[f], wu_ref[:, columns(f)])
        act, slope = gelu_pair(pre)
        h_ref[:, columns(f)] = act.astype(jnp.bfloat16)
        slope_ref[:, columns(f)] = slope
        return 0

    def grad_step(f, _):
        grad = dot(g_ref[...] * ed_ref[f], wd_ref[columns(f), :], NT)
        q_ref[:, columns(f)] = (grad * slope_ref[:, columns(f)]).astype(jnp.bfloat16)
        return 0

    def picked(values_ref, bits_ref, d):
        return jnp.concatenate(
            [
                values_ref[:, f * BLOCK : (f + 1) * BLOCK] * bits_ref[f, :, columns(d)]
                for f in range(blocks_f)
            ],
            axis=1,
        )

    def mixed_block(d):
        return dot(picked(h_ref, ed_ref, d), wd_ref[:, columns(d)])

    def input_block(d):
        return dot(picked(q_ref, eu_ref, d), wu_ref[columns(d), :], NT)

    def total(block, part_ref, sib_ref, out_ref, first):
        def fill(owner):
            def one(b, _):
                part_ref[owner, :, columns(b)] = block(owner * blocks_p + b).astype(jnp.bfloat16)
                return 0

            lax.fori_loop(0, blocks_p, one, 0)

        sent = []
        for n, side in enumerate((1 - x, x)):
            owner = 2 * side + 1 - core
            fill(owner)
            sent += launch([
                remote(part_ref.at[owner], sib_ref.at[side], first + n, {"tensor": sibling})
            ])
        fill(across)
        arrive(sent[:1])
        out_ref[...] = (
            part_ref[across].astype(jnp.float32) + sib_ref[1 - x].astype(jnp.float32)
        ).astype(jnp.bfloat16)
        return fill, sent[1:]

    def cross(out_ref, in_ref, first):
        return launch([remote(out_ref, in_ref, first + 2, {"tensor": across})])

    def send_home(part_ref, sib_ref, in_ref, back, home, first):
        summed = (
            part_ref[t].astype(jnp.float32)
            + sib_ref[x].astype(jnp.float32)
            + in_ref[...].astype(jnp.float32)
        )
        for i in range(groups):
            back[i] = stacked(summed, i * capacity, capacity)
        home[me] = back[me]
        return launch([
            remote(back.at[j], home.at[me], first + k, {"dp": j}) for k, j in enumerate(others)
        ])

    def finish(home, result_ref):
        for i in range(groups):
            unstack(home[i], wide_ref, i * capacity, 0, capacity)
        result_ref[...] = dot(placer_turned, wide_ref[:, :part].astype(jnp.bfloat16)).astype(jnp.bfloat16)

    lax.fori_loop(0, half, pre_step, 0)
    arrive(share_b[:1])
    forward_b = forward(got_b, base + 3)
    lax.fori_loop(half, blocks_f, pre_step, 0)
    load_down.wait()
    fill_m, late_m = total(mixed_block, part_m, sib_m, out_m, base + 6)
    cross_m = cross(out_m, in_m, base + 6)
    fill_m(t)
    arrive(share_b[1:] + forward_b)
    assemble(got_b, g_ref)
    lax.fori_loop(0, blocks_f, grad_step, 0)
    arrive(late_m + cross_m)
    home_trip_m = send_home(part_m, sib_m, in_m, back_m, home_m, base + 12)
    fill_i, late_i = total(input_block, part_i, sib_i, out_i, base + 9)
    cross_i = cross(out_i, in_i, base + 9)
    fill_i(t)
    arrive(late_i + cross_i)
    home_trip_i = send_home(part_i, sib_i, in_i, back_i, home_i, base + 12 + step)
    arrive(home_trip_m)
    finish(home_m, mixed_ref)
    arrive(home_trip_i)
    finish(home_i, grads_ref)
    for copy in every:
        copy.wait_send()


def layer(tokens, cotangent, pair_row, up_table, down_table, up_weight, down_weight, groups, capacity, sides):
    part = tokens.shape[1]
    slots = groups * capacity
    width = part * sides
    hidden = up_weight.shape[1]
    blocks_f = hidden // BLOCK
    lanes = up_table.shape[2]
    tall = capacity * part // BLOCK
    short = -(-capacity // 16) * 16
    vmem = pl.BlockSpec(memory_space=pltpu.VMEM)
    anywhere = pl.BlockSpec(memory_space=pl.ANY)
    trips = 5 * (groups - 1) + 12

    def buffer(*shape):
        return pltpu.VMEM(shape, jnp.bfloat16)

    return pl.pallas_call(
        functools.partial(layer_kernel, groups, capacity),
        out_shape=[jax.ShapeDtypeStruct(tokens.shape, jnp.bfloat16)] * 2,
        in_specs=[vmem] * 5 + [anywhere] * 2,
        out_specs=[vmem] * 2,
        scratch_shapes=[
            buffer(*up_weight.shape),
            buffer(*down_weight.shape),
            buffer(blocks_f, slots, width),
            buffer(blocks_f, slots, width),
            buffer(groups, short, lanes),
            buffer(groups, tall, BLOCK),
            buffer(groups, tall, BLOCK),
            buffer(groups, short, lanes),
            buffer(sides, groups, tall, BLOCK),
            buffer(sides, groups, tall, BLOCK),
            pltpu.VMEM((slots, width), jnp.float32),
            buffer(slots, width),
            buffer(slots, width),
            buffer(slots, hidden),
            buffer(slots, hidden),
            pltpu.VMEM((slots, hidden), jnp.float32),
            buffer(sides, slots, part),
            buffer(sides, slots, part),
            buffer(2, slots, part),
            buffer(2, slots, part),
            buffer(slots, part),
            buffer(slots, part),
            buffer(slots, part),
            buffer(slots, part),
            buffer(groups, tall, BLOCK),
            buffer(groups, tall, BLOCK),
            buffer(groups, tall, BLOCK),
            buffer(groups, tall, BLOCK),
            pltpu.SemaphoreType.DMA((2,)),
            pltpu.SemaphoreType.DMA((trips,)),
            pltpu.SemaphoreType.DMA((trips,)),
        ],
        compiler_params=pltpu.CompilerParams(
            collective_id=0, has_side_effects=True, vmem_limit_bytes=60 * 2**20
        ),
        name="layer",
    )(tokens, cotangent, pair_row, up_table, down_table, up_weight, down_weight)


def place(pair_ids, groups, capacity):
    target = pair_ids % groups
    matches = (target[:, None] == jnp.arange(groups, dtype=jnp.int32)[None, :]).astype(jnp.int32)
    before = jnp.sum((jnp.cumsum(matches, axis=0) - matches) * matches, axis=1)
    position = target * capacity + before
    slots = jnp.arange(groups * capacity, dtype=jnp.int32)
    return (position[None, :] == slots[:, None]).astype(jnp.bfloat16)


def swap(values, groups, capacity):
    width = values.shape[1]
    moved = lax.all_to_all(
        values.reshape(groups, capacity, width), "dp", split_axis=0, concat_axis=0, tiled=True
    )
    return moved.reshape(groups * capacity, width)


def per_device(tokens, cotangent, pair_ids, up_mask, down_mask, up_weight, down_weight):
    groups = lax.axis_size("dp")
    tok_count, part = tokens.shape
    pairs = up_mask.shape[0]
    capacity = max(2, (3 * tok_count + 2 * groups - 1) // (2 * groups))
    slot_count = groups * capacity
    lanes = -(-pairs // BLOCK) * BLOCK
    pad = ((0, 0), (0, 0), (0, lanes - pairs))
    up_table = jnp.pad(jnp.transpose(up_mask, (1, 2, 0)), pad)
    down_table = jnp.pad(jnp.transpose(down_mask, (1, 2, 0)), pad)
    sides = lax.axis_size("tensor")
    if sides == 4 and capacity * part // BLOCK % 16 == 0 and capacity % 8 == 0:
        return layer(
            tokens, cotangent, pair_ids.reshape(1, tok_count), up_table, down_table, up_weight,
            down_weight[0], groups, capacity, sides,
        )

    placer = place(pair_ids, groups, capacity)
    known = (pair_ids[:, None] == jnp.arange(lanes, dtype=jnp.int32)[None, :]).astype(jnp.bfloat16)
    leaving = jnp.concatenate([tokens, cotangent, known], axis=1)
    moved = swap(dot(placer, leaving).astype(jnp.bfloat16), groups, capacity)
    both = jnp.stack([moved[:, :part], moved[:, part : 2 * part]])
    whole = lax.all_gather(both, "tensor", axis=2, tiled=True)
    mixed_part, input_part = compute(
        whole[0], whole[1], moved[:, 2 * part :], up_table, down_table, up_weight, down_weight[0]
    )
    summed = lax.psum_scatter(
        jnp.stack([mixed_part, input_part]), "tensor", scatter_dimension=2, tiled=True
    )
    back = swap(jnp.concatenate([summed[0], summed[1]], axis=1), groups, capacity)
    out = lax.dot_general(
        placer, back, (((0,), (0,)), ((), ())), preferred_element_type=jnp.float32
    ).astype(jnp.bfloat16)
    return out[:, :part], out[:, part:]


def solution(mesh):
    return jax.shard_map(
        per_device,
        mesh=mesh,
        in_specs=(
            P("dp", "tensor"),
            P("dp", "tensor"),
            P("dp"),
            P(None, None, "tensor"),
            P(None, "tensor", None),
            P(None, "tensor"),
            P("dp", "tensor", None),
        ),
        out_specs=(P("dp", "tensor"), P("dp", "tensor")),
        check_vma=False,
    )
```

```python
import functools

import jax
import jax.numpy as jnp
from jax import lax
from jax.experimental import pallas as pl
from jax.experimental.pallas import tpu as pltpu
from jax.sharding import PartitionSpec as P

BLOCK = 128
ROOT = 0.7978845608028654
CUBE = 0.044715
NT = (((1,), (1,)), ((), ()))
NN = (((1,), (0,)), ((), ()))


def dot(a, b, dims=NN):
    return lax.dot_general(a, b, dims, preferred_element_type=jnp.float32)


def gelu_pair(v):
    square = v * v
    t = jnp.tanh(ROOT * (v + CUBE * v * square))
    half = 0.5 * (1.0 + t)
    slope = half + 0.5 * v * (1.0 - t * t) * (ROOT * (1.0 + 3.0 * CUBE * square))
    return v * half, slope


def masked(values_ref, bits, blocks):
    rows = values_ref.shape[0]
    parts = []
    for b in range(blocks):
        own = jnp.broadcast_to(bits[:, b : b + 1], (rows, BLOCK))
        parts.append(values_ref[:, b * BLOCK : (b + 1) * BLOCK] * own)
    return jnp.concatenate(parts, axis=1)


def products(x_ref, g_ref, pick, up_ref, down_ref, wu_ref, wd_ref, h_ref, q_ref, mixed_ref, input_ref):
    blocks_d, blocks_f = up_ref.shape[0], up_ref.shape[1]

    def first(f, _):
        at = pl.ds(pl.multiple_of(f * BLOCK, BLOCK), BLOCK)
        up_bits = dot(pick, up_ref[:, f, :].astype(jnp.bfloat16), NT).astype(jnp.bfloat16)
        down_bits = dot(pick, down_ref[f].astype(jnp.bfloat16), NT).astype(jnp.bfloat16)
        pre = dot(masked(x_ref, up_bits, blocks_d), wu_ref[:, at])
        grad = dot(masked(g_ref, down_bits, blocks_d), wd_ref[at, :], NT)
        act, slope = gelu_pair(pre)
        h_ref[:, at] = act.astype(jnp.bfloat16)
        q_ref[:, at] = (grad * slope).astype(jnp.bfloat16)
        return 0

    def second(d, _):
        at = pl.ds(pl.multiple_of(d * BLOCK, BLOCK), BLOCK)
        up_bits = dot(pick, up_ref[d].astype(jnp.bfloat16), NT).astype(jnp.bfloat16)
        down_bits = dot(pick, down_ref[:, d, :].astype(jnp.bfloat16), NT).astype(jnp.bfloat16)
        mixed_ref[:, at] = dot(masked(h_ref, down_bits, blocks_f), wd_ref[:, at]).astype(jnp.bfloat16)
        input_ref[:, at] = dot(masked(q_ref, up_bits, blocks_f), wu_ref[at, :], NT).astype(jnp.bfloat16)
        return 0

    lax.fori_loop(0, blocks_f, first, 0)
    lax.fori_loop(0, blocks_d, second, 0)


def compute_kernel(x_ref, g_ref, pick_ref, up_ref, down_ref, wu_hbm, wd_hbm, mixed_ref, input_ref,
                   wu_ref, wd_ref, h_ref, q_ref, sems):
    load_up = pltpu.make_async_copy(wu_hbm, wu_ref, sems.at[0])
    load_down = pltpu.make_async_copy(wd_hbm, wd_ref, sems.at[1])
    load_up.start()
    load_down.start()
    load_up.wait()
    load_down.wait()
    products(x_ref, g_ref, pick_ref[...], up_ref, down_ref, wu_ref, wd_ref, h_ref, q_ref, mixed_ref, input_ref)


def compute(x, g, pick, up_table, down_table, up_weight, down_weight):
    rows, width = x.shape
    hidden = up_weight.shape[1]
    vmem = pl.BlockSpec(memory_space=pltpu.VMEM)
    anywhere = pl.BlockSpec(memory_space=pl.ANY)
    return pl.pallas_call(
        compute_kernel,
        out_shape=[jax.ShapeDtypeStruct((rows, width), jnp.bfloat16)] * 2,
        in_specs=[vmem] * 5 + [anywhere] * 2,
        out_specs=[vmem] * 2,
        scratch_shapes=[
            pltpu.VMEM(up_weight.shape, jnp.bfloat16),
            pltpu.VMEM(down_weight.shape, jnp.bfloat16),
            pltpu.VMEM((rows, hidden), jnp.bfloat16),
            pltpu.VMEM((rows, hidden), jnp.bfloat16),
            pltpu.SemaphoreType.DMA((2,)),
        ],
        compiler_params=pltpu.CompilerParams(vmem_limit_bytes=44 * 2**20),
        name="masked_products",
    )(x, g, pick, up_table, down_table, up_weight, down_weight)


MESH = pl.DeviceIdType.MESH


def stacked(values, row, count):
    wide = values.shape[1] // BLOCK
    return jnp.concatenate(
        [values[row : row + count, b * BLOCK : (b + 1) * BLOCK] for b in range(wide)], axis=0
    ).astype(jnp.bfloat16)


def unstack(slab, into_ref, row, column, count):
    wide = slab.astype(jnp.float32)
    for b in range(slab.shape[0] // count):
        into_ref[row : row + count, column + b * BLOCK : column + (b + 1) * BLOCK] = wide[
            b * count : (b + 1) * count
        ]


def layer_kernel(groups, capacity, tokens_ref, pairs_ref, cotangent_hbm, up_hbm, down_hbm, wu_hbm, wd_hbm,
                 rows_ref, turned_ref,
                 wu_ref, wd_ref, up_ref, down_ref, cotangent_ref, eu_ref, ed_ref,
                 send_p, send_a, send_b, got_p, got_a, got_b,
                 wide_ref, x_ref, g_ref, h_ref, q_ref, slope_ref,
                 part_m, part_i, sib_m, sib_i, out_m, out_i, in_m, in_i,
                 back_m, back_i, home_m, home_i, local_sems, ss, rs):
    slots = groups * capacity
    blocks_d, blocks_f = up_ref.shape[0], up_ref.shape[1]
    tok_count, part = tokens_ref.shape
    chunks, chunk = part_m.shape[0], part_m.shape[3]
    blocks_p, blocks_c = part // BLOCK, chunk // BLOCK
    pair_count = up_ref.shape[2]
    lanes = send_p.shape[2]
    me, t = lax.axis_index("dp"), lax.axis_index("tensor")
    core, x = t % 2, t // 2
    sibling, across = 2 * x + 1 - core, 2 * (1 - x) + core
    others = [(me + k) % groups for k in range(1, groups)]

    load_up = pltpu.make_async_copy(wu_hbm, wu_ref, local_sems.at[0])
    load_down = pltpu.make_async_copy(wd_hbm, wd_ref, local_sems.at[1])
    load_ut = pltpu.make_async_copy(up_hbm, up_ref, local_sems.at[2])
    load_dt = pltpu.make_async_copy(down_hbm, down_ref, local_sems.at[3])
    load_cot = pltpu.make_async_copy(cotangent_hbm, cotangent_ref, local_sems.at[4])
    load_ut.start()
    load_dt.start()
    load_cot.start()
    load_up.start()
    load_down.start()

    barrier = pltpu.get_barrier_semaphore()
    for j in others:
        pl.semaphore_signal(barrier, inc=1, device_id={"dp": j}, device_id_type=MESH)
    for s in (sibling, across):
        pl.semaphore_signal(barrier, inc=1, device_id={"tensor": s}, device_id_type=MESH)

    pairs = pairs_ref[...]
    target = lax.rem(pairs, jnp.full_like(pairs, groups))
    group_of = lax.broadcasted_iota(jnp.int32, (groups, tok_count), 0)
    match = group_of == target
    earlier = (
        lax.broadcasted_iota(jnp.int32, (tok_count, tok_count), 0)
        < lax.broadcasted_iota(jnp.int32, (tok_count, tok_count), 1)
    ).astype(jnp.float32).astype(jnp.bfloat16)
    before = dot(match.astype(jnp.float32).astype(jnp.bfloat16), earlier)
    spot = before + (group_of * capacity).astype(jnp.float32)
    position = jnp.sum(jnp.where(match, spot, 0.0), axis=0, keepdims=True)
    slot_of = lax.broadcasted_iota(jnp.int32, (slots, tok_count), 0).astype(jnp.float32)
    placed = (slot_of == position).astype(jnp.float32)
    placer = placed.astype(jnp.bfloat16)
    turned_ref[...] = placed.T.astype(jnp.bfloat16)
    known = (lax.broadcasted_iota(jnp.int32, (lanes, tok_count), 0) == pairs).astype(jnp.float32)
    moved = dot(placer, known.astype(jnp.bfloat16), NT)
    room = send_p.shape[1] - capacity
    for j in range(groups):
        own = moved[j * capacity : (j + 1) * capacity]
        if room:
            own = jnp.concatenate([own, jnp.zeros((room, lanes), jnp.float32)], axis=0)
        send_p[j] = own.astype(jnp.bfloat16)
    got_p[me] = send_p[me]

    pl.semaphore_wait(barrier, groups + 1)

    def remote(src, dst, sem, where):
        return pltpu.make_async_remote_copy(
            src_ref=src, dst_ref=dst, send_sem=ss.at[sem], recv_sem=rs.at[sem],
            device_id=where, device_id_type=MESH,
        )

    step = groups - 1
    every = []

    def launch(copies):
        for copy in copies:
            copy.start()
        every.extend(copies)
        return copies

    def arrive(copies):
        for copy in copies:
            copy.wait_recv()

    trip_p = launch([
        remote(send_p.at[j], got_p.at[me], k, {"dp": j}) for k, j in enumerate(others)
    ])

    def dispatch(values_ref, send, got, first):
        moved = dot(placer, values_ref[...])
        for j in range(groups):
            send[j] = stacked(moved, j * capacity, capacity)
        got[t, me] = send[me]
        return launch([
            remote(send.at[j], got.at[t, me], first + k, {"dp": j}) for k, j in enumerate(others)
        ])

    trip_a = dispatch(tokens_ref, send_a, got_a, step)
    base = 3 * step

    def share(got, first):
        return launch([
            remote(got.at[t], got.at[t], first, {"tensor": across}),
            remote(got.at[t], got.at[t], first + 1, {"tensor": sibling}),
        ])

    def forward(got, first):
        return launch([remote(got.at[across], got.at[across], first + 2, {"tensor": sibling})])

    arrive(trip_p)
    for i in range(groups):
        unstack(got_p[i, :capacity], wide_ref, i * capacity, 0, capacity)
    pick = wide_ref[:, :pair_count].astype(jnp.bfloat16)
    load_ut.wait()
    load_dt.wait()
    load_cot.wait()

    def expand(table, into_ref, f):
        bits = dot(pick, table.astype(jnp.float32).astype(jnp.bfloat16), NT).astype(jnp.bfloat16)
        for d in range(blocks_d):
            into_ref[f, :, d * BLOCK : (d + 1) * BLOCK] = jnp.broadcast_to(
                bits[:, d : d + 1], (slots, BLOCK)
            )

    def steps(low, high, at_once, one):
        def several(n, _):
            for k in range(at_once):
                one(low + n * at_once + k)
            return 0

        lax.fori_loop(0, (high - low) // at_once, several, 0)

    half = blocks_f // 2
    steps(0, blocks_f, 2, lambda f: expand(up_ref[:, f, :], eu_ref, f))
    arrive(trip_a)
    share_a = share(got_a, base)
    trip_b = dispatch(cotangent_ref, send_b, got_b, 2 * step)
    steps(0, half, 2, lambda f: expand(down_ref[f], ed_ref, f))
    arrive(share_a[:1])
    forward_a = forward(got_a, base)
    steps(half, blocks_f, 2, lambda f: expand(down_ref[f], ed_ref, f))
    arrive(share_a[1:] + forward_a)

    def assemble(got, into_ref):
        for s in range(got.shape[0]):
            for i in range(groups):
                unstack(got[s, i], wide_ref, i * capacity, s * part, capacity)
        into_ref[...] = wide_ref[...].astype(jnp.bfloat16)

    assemble(got_a, x_ref)
    load_up.wait()

    def columns(b):
        return pl.ds(pl.multiple_of(b * BLOCK, BLOCK), BLOCK)

    def pre_step(f):
        pre = dot(x_ref[...] * eu_ref[f], wu_ref[:, columns(f)])
        act, slope = gelu_pair(pre)
        h_ref[:, columns(f)] = act.astype(jnp.bfloat16)
        slope_ref[:, columns(f)] = slope

    def grad_step(f):
        grad = dot(g_ref[...] * ed_ref[f], wd_ref[columns(f), :], NT)
        q_ref[:, columns(f)] = (grad * slope_ref[:, columns(f)]).astype(jnp.bfloat16)

    def picked(values_ref, bits_ref, d):
        return jnp.concatenate(
            [
                values_ref[:, f * BLOCK : (f + 1) * BLOCK] * bits_ref[f, :, columns(d)]
                for f in range(blocks_f)
            ],
            axis=1,
        )

    def mixed_block(d):
        return dot(picked(h_ref, ed_ref, d), wd_ref[:, columns(d)])

    def input_block(d):
        return dot(picked(q_ref, eu_ref, d), wu_ref[columns(d), :], NT)

    class Sums:
        def __init__(self, block, part_ref, sib_ref, out_ref, in_ref, back_ref, home_ref, first):
            self.block, self.part, self.sib, self.out = block, part_ref, sib_ref, out_ref
            self.into, self.back, self.home, self.first = in_ref, back_ref, home_ref, first

        def to_sibling(self, h, n):
            side = (1 - x, x)[n]
            return remote(
                self.part.at[h, 2 * side + 1 - core], self.sib.at[h, side],
                self.first + h * (3 + step) + n, {"tensor": sibling},
            )

        def to_across(self, h):
            return remote(
                self.out.at[h], self.into.at[h], self.first + h * (3 + step) + 2, {"tensor": across}
            )

        def to_home(self, h):
            return [
                remote(
                    self.back.at[h, j], self.home.at[h, me],
                    self.first + h * (3 + step) + 3 + k, {"dp": j},
                )
                for k, j in enumerate(others)
            ]

        def fill(self, h, owner):
            for b in range(blocks_c):
                d = owner * blocks_p + h * blocks_c + b
                self.part[h, owner, :, b * BLOCK : (b + 1) * BLOCK] = self.block(d).astype(jnp.bfloat16)

        def launch_home(self, h):
            self.to_sibling(h, 1).wait_recv()
            self.to_across(h).wait_recv()
            summed = (
                self.part[h, t].astype(jnp.float32)
                + self.sib[h, x].astype(jnp.float32)
                + self.into[h].astype(jnp.float32)
            )
            for i in range(groups):
                self.back[h, i] = stacked(summed, i * capacity, capacity)
            self.home[h, me] = self.back[h, me]
            for copy in self.to_home(h):
                copy.start()

        def run(self, hook):
            def one(h, _):
                self.fill(h, 2 * (1 - x) + 1 - core)
                self.to_sibling(h, 0).start()

                @pl.when(h > 0)
                def _():
                    hook()
                    self.launch_home(h - 1)

                self.fill(h, across)
                self.to_sibling(h, 0).wait_recv()
                self.out[h] = (
                    self.part[h, across].astype(jnp.float32) + self.sib[h, 1 - x].astype(jnp.float32)
                ).astype(jnp.bfloat16)
                self.to_across(h).start()
                self.fill(h, 2 * x + 1 - core)
                self.to_sibling(h, 1).start()
                self.fill(h, t)
                return 0

            lax.fori_loop(0, chunks, one, 0)

        def finish(self, n):
            for h in range(chunks):
                for copy in self.to_home(h):
                    copy.wait_recv()
                for i in range(groups):
                    unstack(self.home[h, i], wide_ref, i * capacity, h * chunk, capacity)
            rows_ref[n] = wide_ref[:, :part].astype(jnp.bfloat16)

        def settle(self):
            for h in range(chunks):
                for copy in [self.to_sibling(h, 0), self.to_sibling(h, 1), self.to_across(h)] + self.to_home(h):
                    copy.wait_send()

    sums_m = Sums(mixed_block, part_m, sib_m, out_m, in_m, back_m, home_m, base + 6)
    sums_i = Sums(
        input_block, part_i, sib_i, out_i, in_i, back_i, home_i, base + 6 + chunks * (3 + step)
    )

    steps(0, half, 4, pre_step)
    arrive(trip_b)
    share_b = share(got_b, base + 3)
    steps(half, blocks_f, 4, pre_step)
    load_down.wait()
    forward_b = remote(got_b.at[across], got_b.at[across], base + 5, {"tensor": sibling})

    def pass_on():
        share_b[0].wait_recv()
        forward_b.start()

    sums_m.run(pass_on)
    share_b[1].wait_recv()
    forward_b.wait_recv()
    assemble(got_b, g_ref)
    steps(0, half, 4, grad_step)
    sums_m.launch_home(chunks - 1)
    steps(half, blocks_f, 4, grad_step)
    sums_i.run(lambda: None)
    sums_i.launch_home(chunks - 1)
    sums_m.finish(0)
    sums_i.finish(1)
    for copy in every:
        copy.wait_send()
    forward_b.wait_send()
    sums_m.settle()
    sums_i.settle()


def settle_kernel(rows_ref, turned_ref, mixed_ref, grads_ref):
    turned = turned_ref[...]
    mixed_ref[...] = dot(turned, rows_ref[0]).astype(jnp.bfloat16)
    grads_ref[...] = dot(turned, rows_ref[1]).astype(jnp.bfloat16)


def layer(tokens, cotangent, pair_row, up_table, down_table, up_weight, down_weight, groups, capacity, sides):
    part = tokens.shape[1]
    slots = groups * capacity
    width = part * sides
    hidden = up_weight.shape[1]
    blocks_f = hidden // BLOCK
    lanes = -(-up_table.shape[2] // BLOCK) * BLOCK
    chunks = 2
    chunk = part // chunks
    tall = capacity * part // BLOCK
    short = -(-capacity // 16) * 16
    vmem = pl.BlockSpec(memory_space=pltpu.VMEM)
    anywhere = pl.BlockSpec(memory_space=pl.ANY)
    trips = 3 * (groups - 1) + 6 + 2 * chunks * (groups + 2)

    def buffer(*shape):
        return pltpu.VMEM(shape, jnp.bfloat16)

    rows, turned = pl.pallas_call(
        functools.partial(layer_kernel, groups, capacity),
        out_shape=[
            jax.ShapeDtypeStruct((2, slots, part), jnp.bfloat16),
            jax.ShapeDtypeStruct((tokens.shape[0], slots), jnp.bfloat16),
        ],
        in_specs=[vmem] * 2 + [anywhere] * 5,
        out_specs=[vmem] * 2,
        scratch_shapes=[
            buffer(*up_weight.shape),
            buffer(*down_weight.shape),
            pltpu.VMEM(up_table.shape, jnp.int32),
            pltpu.VMEM(down_table.shape, jnp.int32),
            buffer(*cotangent.shape),
            buffer(blocks_f, slots, width),
            buffer(blocks_f, slots, width),
            buffer(groups, short, lanes),
            buffer(groups, tall, BLOCK),
            buffer(groups, tall, BLOCK),
            buffer(groups, short, lanes),
            buffer(sides, groups, tall, BLOCK),
            buffer(sides, groups, tall, BLOCK),
            pltpu.VMEM((slots, width), jnp.float32),
            buffer(slots, width),
            buffer(slots, width),
            buffer(slots, hidden),
            buffer(slots, hidden),
            pltpu.VMEM((slots, hidden), jnp.float32),
            buffer(chunks, sides, slots, chunk),
            buffer(chunks, sides, slots, chunk),
            buffer(chunks, 2, slots, chunk),
            buffer(chunks, 2, slots, chunk),
            buffer(chunks, slots, chunk),
            buffer(chunks, slots, chunk),
            buffer(chunks, slots, chunk),
            buffer(chunks, slots, chunk),
            buffer(chunks, groups, tall // chunks, BLOCK),
            buffer(chunks, groups, tall // chunks, BLOCK),
            buffer(chunks, groups, tall // chunks, BLOCK),
            buffer(chunks, groups, tall // chunks, BLOCK),
            pltpu.SemaphoreType.DMA((5,)),
            pltpu.SemaphoreType.DMA((trips,)),
            pltpu.SemaphoreType.DMA((trips,)),
        ],
        compiler_params=pltpu.CompilerParams(
            collective_id=0, has_side_effects=True, vmem_limit_bytes=60 * 2**20
        ),
        name="layer",
    )(tokens, pair_row, cotangent, up_table, down_table, up_weight, down_weight)
    return pl.pallas_call(
        settle_kernel,
        out_shape=[jax.ShapeDtypeStruct(tokens.shape, jnp.bfloat16)] * 2,
        in_specs=[vmem] * 2,
        out_specs=[vmem] * 2,
        name="settle",
    )(rows, turned)


def place(pair_ids, groups, capacity):
    target = pair_ids % groups
    matches = (target[:, None] == jnp.arange(groups, dtype=jnp.int32)[None, :]).astype(jnp.int32)
    before = jnp.sum((jnp.cumsum(matches, axis=0) - matches) * matches, axis=1)
    position = target * capacity + before
    slots = jnp.arange(groups * capacity, dtype=jnp.int32)
    return (position[None, :] == slots[:, None]).astype(jnp.bfloat16)


def swap(values, groups, capacity):
    width = values.shape[1]
    moved = lax.all_to_all(
        values.reshape(groups, capacity, width), "dp", split_axis=0, concat_axis=0, tiled=True
    )
    return moved.reshape(groups * capacity, width)


def per_device(tokens, cotangent, pair_ids, up_mask, down_mask, up_weight, down_weight):
    groups = lax.axis_size("dp")
    tok_count, part = tokens.shape
    pairs = up_mask.shape[0]
    capacity = max(2, (3 * tok_count + 2 * groups - 1) // (2 * groups))
    slot_count = groups * capacity
    lanes = -(-pairs // BLOCK) * BLOCK
    pad = ((0, 0), (0, 0), (0, lanes - pairs))
    up_table = jnp.transpose(up_mask, (1, 2, 0))
    down_table = jnp.transpose(down_mask, (1, 2, 0))
    sides = lax.axis_size("tensor")
    if sides == 4 and part % 256 == 0 and capacity * part // 256 % 16 == 0 and capacity % 8 == 0:
        return layer(
            tokens, cotangent, pair_ids.reshape(1, tok_count), up_table, down_table, up_weight,
            down_weight[0], groups, capacity, sides,
        )

    placer = place(pair_ids, groups, capacity)
    known = (pair_ids[:, None] == jnp.arange(lanes, dtype=jnp.int32)[None, :]).astype(jnp.bfloat16)
    leaving = jnp.concatenate([tokens, cotangent, known], axis=1)
    moved = swap(dot(placer, leaving).astype(jnp.bfloat16), groups, capacity)
    both = jnp.stack([moved[:, :part], moved[:, part : 2 * part]])
    whole = lax.all_gather(both, "tensor", axis=2, tiled=True)
    mixed_part, input_part = compute(
        whole[0], whole[1], moved[:, 2 * part :], jnp.pad(up_table, pad), jnp.pad(down_table, pad), up_weight, down_weight[0]
    )
    summed = lax.psum_scatter(
        jnp.stack([mixed_part, input_part]), "tensor", scatter_dimension=2, tiled=True
    )
    back = swap(jnp.concatenate([summed[0], summed[1]], axis=1), groups, capacity)
    out = lax.dot_general(
        placer, back, (((0,), (0,)), ((), ())), preferred_element_type=jnp.float32
    ).astype(jnp.bfloat16)
    return out[:, :part], out[:, part:]


def solution(mesh):
    return jax.shard_map(
        per_device,
        mesh=mesh,
        in_specs=(
            P("dp", "tensor"),
            P("dp", "tensor"),
            P("dp"),
            P(None, None, "tensor"),
            P(None, "tensor", None),
            P(None, "tensor"),
            P("dp", "tensor", None),
        ),
        out_specs=(P("dp", "tensor"), P("dp", "tensor")),
        check_vma=False,
    )
```

```python
import functools

import jax
import jax.numpy as jnp
from jax import lax
from jax.experimental import pallas as pl
from jax.experimental.pallas import tpu as pltpu
from jax.sharding import PartitionSpec as P

BLOCK = 128
TILE = 256
ROOT = 0.7978845608028654
CUBE = 0.044715
NT = (((1,), (1,)), ((), ()))
NN = (((1,), (0,)), ((), ()))


def dot(a, b, dims=NN):
    return lax.dot_general(a, b, dims, preferred_element_type=jnp.float32)


def gelu_pair(v):
    square = v * v
    t = jnp.tanh(ROOT * (v + CUBE * v * square))
    half = 0.5 * (1.0 + t)
    slope = half + 0.5 * v * (1.0 - t * t) * (ROOT * (1.0 + 3.0 * CUBE * square))
    return v * half, slope


def masked(values_ref, bits, blocks):
    rows = values_ref.shape[0]
    parts = []
    for b in range(blocks):
        own = jnp.broadcast_to(bits[:, b : b + 1], (rows, BLOCK))
        parts.append(values_ref[:, b * BLOCK : (b + 1) * BLOCK] * own)
    return jnp.concatenate(parts, axis=1)


def products(x_ref, g_ref, pick, up_ref, down_ref, wu_ref, wd_ref, h_ref, q_ref, mixed_ref, input_ref):
    blocks_d, blocks_f = up_ref.shape[0], up_ref.shape[1]

    def first(f, _):
        at = pl.ds(pl.multiple_of(f * BLOCK, BLOCK), BLOCK)
        up_bits = dot(pick, up_ref[:, f, :].astype(jnp.bfloat16), NT).astype(jnp.bfloat16)
        down_bits = dot(pick, down_ref[f].astype(jnp.bfloat16), NT).astype(jnp.bfloat16)
        pre = dot(masked(x_ref, up_bits, blocks_d), wu_ref[:, at])
        grad = dot(masked(g_ref, down_bits, blocks_d), wd_ref[at, :], NT)
        act, slope = gelu_pair(pre)
        h_ref[:, at] = act.astype(jnp.bfloat16)
        q_ref[:, at] = (grad * slope).astype(jnp.bfloat16)
        return 0

    def second(d, _):
        at = pl.ds(pl.multiple_of(d * BLOCK, BLOCK), BLOCK)
        up_bits = dot(pick, up_ref[d].astype(jnp.bfloat16), NT).astype(jnp.bfloat16)
        down_bits = dot(pick, down_ref[:, d, :].astype(jnp.bfloat16), NT).astype(jnp.bfloat16)
        mixed_ref[:, at] = dot(masked(h_ref, down_bits, blocks_f), wd_ref[:, at]).astype(jnp.bfloat16)
        input_ref[:, at] = dot(masked(q_ref, up_bits, blocks_f), wu_ref[at, :], NT).astype(jnp.bfloat16)
        return 0

    lax.fori_loop(0, blocks_f, first, 0)
    lax.fori_loop(0, blocks_d, second, 0)


def compute_kernel(x_ref, g_ref, pick_ref, up_ref, down_ref, wu_hbm, wd_hbm, mixed_ref, input_ref,
                   wu_ref, wd_ref, h_ref, q_ref, sems):
    load_up = pltpu.make_async_copy(wu_hbm, wu_ref, sems.at[0])
    load_down = pltpu.make_async_copy(wd_hbm, wd_ref, sems.at[1])
    load_up.start()
    load_down.start()
    load_up.wait()
    load_down.wait()
    products(x_ref, g_ref, pick_ref[...], up_ref, down_ref, wu_ref, wd_ref, h_ref, q_ref, mixed_ref, input_ref)


def compute(x, g, pick, up_table, down_table, up_weight, down_weight):
    rows, width = x.shape
    hidden = up_weight.shape[1]
    vmem = pl.BlockSpec(memory_space=pltpu.VMEM)
    anywhere = pl.BlockSpec(memory_space=pl.ANY)
    return pl.pallas_call(
        compute_kernel,
        out_shape=[jax.ShapeDtypeStruct((rows, width), jnp.bfloat16)] * 2,
        in_specs=[vmem] * 5 + [anywhere] * 2,
        out_specs=[vmem] * 2,
        scratch_shapes=[
            pltpu.VMEM(up_weight.shape, jnp.bfloat16),
            pltpu.VMEM(down_weight.shape, jnp.bfloat16),
            pltpu.VMEM((rows, hidden), jnp.bfloat16),
            pltpu.VMEM((rows, hidden), jnp.bfloat16),
            pltpu.SemaphoreType.DMA((2,)),
        ],
        compiler_params=pltpu.CompilerParams(vmem_limit_bytes=44 * 2**20),
        name="masked_products",
    )(x, g, pick, up_table, down_table, up_weight, down_weight)


MESH = pl.DeviceIdType.MESH


def stacked(values, row, count):
    wide = values.shape[1] // BLOCK
    return jnp.concatenate(
        [values[row : row + count, b * BLOCK : (b + 1) * BLOCK] for b in range(wide)], axis=0
    ).astype(jnp.bfloat16)


def unstack(slab, into_ref, row, column, count):
    wide = slab.astype(jnp.float32)
    for b in range(slab.shape[0] // count):
        into_ref[row : row + count, column + b * BLOCK : column + (b + 1) * BLOCK] = wide[
            b * count : (b + 1) * count
        ]


def layer_kernel(groups, capacity, tokens_ref, pairs_ref, cotangent_hbm, up_hbm, down_hbm, wu_hbm, wd_hbm,
                 rows_ref, turned_ref,
                 wu_ref, wd_ref, up_ref, down_ref, cotangent_ref, eu_ref, ed_ref,
                 send_p, send_a, send_b, got_p, got_a, got_b,
                 wide_ref, x_ref, g_ref, h_ref, q_ref, slope_ref,
                 part_m, part_i, sib_m, sib_i, out_m, out_i, in_m, in_i,
                 back_m, back_i, home_m, home_i, local_sems, ss, rs):
    slots = groups * capacity
    blocks_d, blocks_f = up_ref.shape[0], up_ref.shape[1]
    tok_count, part = tokens_ref.shape
    chunks, chunk = part_m.shape[0], part_m.shape[3]
    blocks_p, blocks_c = part // BLOCK, chunk // BLOCK
    pair_count = up_ref.shape[2]
    lanes = send_p.shape[2]
    me, t = lax.axis_index("dp"), lax.axis_index("tensor")
    core, x = t % 2, t // 2
    sibling, across = 2 * x + 1 - core, 2 * (1 - x) + core
    others = [(me + k) % groups for k in range(1, groups)]

    load_up = pltpu.make_async_copy(wu_hbm, wu_ref, local_sems.at[0])
    load_down = pltpu.make_async_copy(wd_hbm, wd_ref, local_sems.at[1])
    load_ut = pltpu.make_async_copy(up_hbm, up_ref, local_sems.at[2])
    load_dt = pltpu.make_async_copy(down_hbm, down_ref, local_sems.at[3])
    load_cot = pltpu.make_async_copy(cotangent_hbm, cotangent_ref, local_sems.at[4])
    load_ut.start()
    load_dt.start()
    load_cot.start()
    load_up.start()
    load_down.start()

    barrier = pltpu.get_barrier_semaphore()
    for j in others:
        pl.semaphore_signal(barrier, inc=1, device_id={"dp": j}, device_id_type=MESH)
    for s in (sibling, across):
        pl.semaphore_signal(barrier, inc=1, device_id={"tensor": s}, device_id_type=MESH)

    pairs = pairs_ref[...]
    target = lax.rem(pairs, jnp.full_like(pairs, groups))
    group_of = lax.broadcasted_iota(jnp.int32, (groups, tok_count), 0)
    match = group_of == target
    earlier = (
        lax.broadcasted_iota(jnp.int32, (tok_count, tok_count), 0)
        < lax.broadcasted_iota(jnp.int32, (tok_count, tok_count), 1)
    ).astype(jnp.float32).astype(jnp.bfloat16)
    before = dot(match.astype(jnp.float32).astype(jnp.bfloat16), earlier)
    spot = before + (group_of * capacity).astype(jnp.float32)
    position = jnp.sum(jnp.where(match, spot, 0.0), axis=0, keepdims=True)
    slot_of = lax.broadcasted_iota(jnp.int32, (slots, tok_count), 0).astype(jnp.float32)
    placed = (slot_of == position).astype(jnp.float32)
    placer = placed.astype(jnp.bfloat16)
    turned_ref[...] = placed.T.astype(jnp.bfloat16)
    known = (lax.broadcasted_iota(jnp.int32, (lanes, tok_count), 0) == pairs).astype(jnp.float32)
    moved = dot(placer, known.astype(jnp.bfloat16), NT)
    room = send_p.shape[1] - capacity
    for j in range(groups):
        own = moved[j * capacity : (j + 1) * capacity]
        if room:
            own = jnp.concatenate([own, jnp.zeros((room, lanes), jnp.float32)], axis=0)
        send_p[j] = own.astype(jnp.bfloat16)
    got_p[me] = send_p[me]

    pl.semaphore_wait(barrier, groups + 1)

    def remote(src, dst, sem, where):
        return pltpu.make_async_remote_copy(
            src_ref=src, dst_ref=dst, send_sem=ss.at[sem], recv_sem=rs.at[sem],
            device_id=where, device_id_type=MESH,
        )

    step = groups - 1
    every = []

    def launch(copies):
        for copy in copies:
            copy.start()
        every.extend(copies)
        return copies

    def arrive(copies):
        for copy in copies:
            copy.wait_recv()

    trip_p = launch([
        remote(send_p.at[j], got_p.at[me], k, {"dp": j}) for k, j in enumerate(others)
    ])

    def dispatch(values_ref, send, got, first):
        moved = dot(placer, values_ref[...])
        for j in range(groups):
            send[j] = stacked(moved, j * capacity, capacity)
        got[t, me] = send[me]
        return launch([
            remote(send.at[j], got.at[t, me], first + k, {"dp": j}) for k, j in enumerate(others)
        ])

    trip_a = dispatch(tokens_ref, send_a, got_a, step)
    base = 3 * step

    def share(got, first):
        return launch([
            remote(got.at[t], got.at[t], first, {"tensor": across}),
            remote(got.at[t], got.at[t], first + 1, {"tensor": sibling}),
        ])

    def forward(got, first):
        return launch([remote(got.at[across], got.at[across], first + 2, {"tensor": sibling})])

    arrive(trip_p)
    for i in range(groups):
        unstack(got_p[i, :capacity], wide_ref, i * capacity, 0, capacity)
    pick = wide_ref[:, :pair_count].astype(jnp.bfloat16)
    load_ut.wait()
    load_dt.wait()
    load_cot.wait()

    def expand(table, into_ref, f):
        bits = dot(pick, table.astype(jnp.float32).astype(jnp.bfloat16), NT).astype(jnp.bfloat16)
        for d in range(blocks_d):
            into_ref[f, :, d * BLOCK : (d + 1) * BLOCK] = jnp.broadcast_to(
                bits[:, d : d + 1], (slots, BLOCK)
            )

    def steps(low, high, at_once, one):
        def several(n, _):
            for k in range(at_once):
                one(low + n * at_once + k)
            return 0

        lax.fori_loop(0, (high - low) // at_once, several, 0)

    half = blocks_f // 2
    steps(0, blocks_f, 2, lambda f: expand(up_ref[:, f, :], eu_ref, f))
    arrive(trip_a)
    share_a = share(got_a, base)
    trip_b = dispatch(cotangent_ref, send_b, got_b, 2 * step)
    steps(0, half, 2, lambda f: expand(down_ref[f], ed_ref, f))
    arrive(share_a[:1])
    forward_a = forward(got_a, base)
    steps(half, blocks_f, 2, lambda f: expand(down_ref[f], ed_ref, f))
    arrive(share_a[1:] + forward_a)

    def assemble(got, into_ref):
        for s in range(got.shape[0]):
            for i in range(groups):
                unstack(got[s, i], wide_ref, i * capacity, s * part, capacity)
        into_ref[...] = wide_ref[...].astype(jnp.bfloat16)

    assemble(got_a, x_ref)
    load_up.wait()

    def columns(b):
        return pl.ds(pl.multiple_of(b * BLOCK, BLOCK), BLOCK)

    def tiled(depth, left, right, dims):
        sums = None
        for k in range(0, depth, TILE):
            one = dot(left(k), right(k), dims)
            sums = one if sums is None else sums + one
        return sums

    def cut(k):
        return slice(k, k + TILE)

    def pre_step(f):
        pre = tiled(
            x_ref.shape[1],
            lambda k: x_ref[:, cut(k)] * eu_ref[f, :, cut(k)],
            lambda k: wu_ref[cut(k), columns(f)],
            NN,
        )
        act, slope = gelu_pair(pre)
        h_ref[:, columns(f)] = act.astype(jnp.bfloat16)
        slope_ref[:, columns(f)] = slope

    def grad_step(f):
        grad = tiled(
            g_ref.shape[1],
            lambda k: g_ref[:, cut(k)] * ed_ref[f, :, cut(k)],
            lambda k: wd_ref[columns(f), cut(k)],
            NT,
        )
        q_ref[:, columns(f)] = (grad * slope_ref[:, columns(f)]).astype(jnp.bfloat16)

    def picked(values_ref, bits_ref, d, k):
        bits = [bits_ref[f, :, columns(d)] for f in range(k // BLOCK, (k + TILE) // BLOCK)]
        return values_ref[:, cut(k)] * jnp.concatenate(bits, axis=1)

    def mixed_block(d):
        return tiled(
            h_ref.shape[1],
            lambda k: picked(h_ref, ed_ref, d, k),
            lambda k: wd_ref[cut(k), columns(d)],
            NN,
        )

    def input_block(d):
        return tiled(
            q_ref.shape[1],
            lambda k: picked(q_ref, eu_ref, d, k),
            lambda k: wu_ref[columns(d), cut(k)],
            NT,
        )

    class Sums:
        def __init__(self, block, part_ref, sib_ref, out_ref, in_ref, back_ref, home_ref, first):
            self.block, self.part, self.sib, self.out = block, part_ref, sib_ref, out_ref
            self.into, self.back, self.home, self.first = in_ref, back_ref, home_ref, first

        def to_sibling(self, h, n):
            side = (1 - x, x)[n]
            return remote(
                self.part.at[h, 2 * side + 1 - core], self.sib.at[h, side],
                self.first + h * (3 + step) + n, {"tensor": sibling},
            )

        def to_across(self, h):
            return remote(
                self.out.at[h], self.into.at[h], self.first + h * (3 + step) + 2, {"tensor": across}
            )

        def to_home(self, h):
            return [
                remote(
                    self.back.at[h, j], self.home.at[h, me],
                    self.first + h * (3 + step) + 3 + k, {"dp": j},
                )
                for k, j in enumerate(others)
            ]

        def fill(self, h, owner):
            for b in range(blocks_c):
                d = owner * blocks_p + h * blocks_c + b
                self.part[h, owner, :, b * BLOCK : (b + 1) * BLOCK] = self.block(d).astype(jnp.bfloat16)

        def launch_home(self, h):
            self.to_sibling(h, 1).wait_recv()
            self.to_across(h).wait_recv()
            summed = (
                self.part[h, t].astype(jnp.float32)
                + self.sib[h, x].astype(jnp.float32)
                + self.into[h].astype(jnp.float32)
            )
            for i in range(groups):
                self.back[h, i] = stacked(summed, i * capacity, capacity)
            self.home[h, me] = self.back[h, me]
            for copy in self.to_home(h):
                copy.start()

        def run(self, hook):
            def one(h, _):
                self.fill(h, 2 * (1 - x) + 1 - core)
                self.to_sibling(h, 0).start()

                @pl.when(h > 0)
                def _():
                    hook()
                    self.launch_home(h - 1)

                self.fill(h, across)
                self.to_sibling(h, 0).wait_recv()
                self.out[h] = (
                    self.part[h, across].astype(jnp.float32) + self.sib[h, 1 - x].astype(jnp.float32)
                ).astype(jnp.bfloat16)
                self.to_across(h).start()
                self.fill(h, 2 * x + 1 - core)
                self.to_sibling(h, 1).start()
                self.fill(h, t)
                return 0

            lax.fori_loop(0, chunks, one, 0)

        def finish(self, n):
            for h in range(chunks):
                for copy in self.to_home(h):
                    copy.wait_recv()
                for i in range(groups):
                    unstack(self.home[h, i], wide_ref, i * capacity, h * chunk, capacity)
            rows_ref[n] = wide_ref[:, :part].astype(jnp.bfloat16)

        def settle(self):
            for h in range(chunks):
                for copy in [self.to_sibling(h, 0), self.to_sibling(h, 1), self.to_across(h)] + self.to_home(h):
                    copy.wait_send()

    sums_m = Sums(mixed_block, part_m, sib_m, out_m, in_m, back_m, home_m, base + 6)
    sums_i = Sums(
        input_block, part_i, sib_i, out_i, in_i, back_i, home_i, base + 6 + chunks * (3 + step)
    )

    steps(0, half, 4, pre_step)
    arrive(trip_b)
    share_b = share(got_b, base + 3)
    steps(half, blocks_f, 4, pre_step)
    load_down.wait()
    forward_b = remote(got_b.at[across], got_b.at[across], base + 5, {"tensor": sibling})

    def pass_on():
        share_b[0].wait_recv()
        forward_b.start()

    sums_m.run(pass_on)
    share_b[1].wait_recv()
    forward_b.wait_recv()
    assemble(got_b, g_ref)
    steps(0, half, 4, grad_step)
    sums_m.launch_home(chunks - 1)
    steps(half, blocks_f, 4, grad_step)
    sums_i.run(lambda: None)
    sums_i.launch_home(chunks - 1)
    sums_m.finish(0)
    sums_i.finish(1)
    for copy in every:
        copy.wait_send()
    forward_b.wait_send()
    sums_m.settle()
    sums_i.settle()


def settle_kernel(rows_ref, turned_ref, mixed_ref, grads_ref):
    turned = turned_ref[...]
    mixed_ref[...] = dot(turned, rows_ref[0]).astype(jnp.bfloat16)
    grads_ref[...] = dot(turned, rows_ref[1]).astype(jnp.bfloat16)


def layer(tokens, cotangent, pair_row, up_table, down_table, up_weight, down_weight, groups, capacity, sides):
    part = tokens.shape[1]
    slots = groups * capacity
    width = part * sides
    hidden = up_weight.shape[1]
    blocks_f = hidden // BLOCK
    lanes = -(-up_table.shape[2] // BLOCK) * BLOCK
    chunks = 2
    chunk = part // chunks
    tall = capacity * part // BLOCK
    short = -(-capacity // 16) * 16
    vmem = pl.BlockSpec(memory_space=pltpu.VMEM)
    anywhere = pl.BlockSpec(memory_space=pl.ANY)
    trips = 3 * (groups - 1) + 6 + 2 * chunks * (groups + 2)

    def buffer(*shape):
        return pltpu.VMEM(shape, jnp.bfloat16)

    rows, turned = pl.pallas_call(
        functools.partial(layer_kernel, groups, capacity),
        out_shape=[
            jax.ShapeDtypeStruct((2, slots, part), jnp.bfloat16),
            jax.ShapeDtypeStruct((tokens.shape[0], slots), jnp.bfloat16),
        ],
        in_specs=[vmem] * 2 + [anywhere] * 5,
        out_specs=[vmem] * 2,
        scratch_shapes=[
            buffer(*up_weight.shape),
            buffer(*down_weight.shape),
            pltpu.VMEM(up_table.shape, jnp.int32),
            pltpu.VMEM(down_table.shape, jnp.int32),
            buffer(*cotangent.shape),
            buffer(blocks_f, slots, width),
            buffer(blocks_f, slots, width),
            buffer(groups, short, lanes),
            buffer(groups, tall, BLOCK),
            buffer(groups, tall, BLOCK),
            buffer(groups, short, lanes),
            buffer(sides, groups, tall, BLOCK),
            buffer(sides, groups, tall, BLOCK),
            pltpu.VMEM((slots, width), jnp.float32),
            buffer(slots, width),
            buffer(slots, width),
            buffer(slots, hidden),
            buffer(slots, hidden),
            pltpu.VMEM((slots, hidden), jnp.float32),
            buffer(chunks, sides, slots, chunk),
            buffer(chunks, sides, slots, chunk),
            buffer(chunks, 2, slots, chunk),
            buffer(chunks, 2, slots, chunk),
            buffer(chunks, slots, chunk),
            buffer(chunks, slots, chunk),
            buffer(chunks, slots, chunk),
            buffer(chunks, slots, chunk),
            buffer(chunks, groups, tall // chunks, BLOCK),
            buffer(chunks, groups, tall // chunks, BLOCK),
            buffer(chunks, groups, tall // chunks, BLOCK),
            buffer(chunks, groups, tall // chunks, BLOCK),
            pltpu.SemaphoreType.DMA((5,)),
            pltpu.SemaphoreType.DMA((trips,)),
            pltpu.SemaphoreType.DMA((trips,)),
        ],
        compiler_params=pltpu.CompilerParams(
            collective_id=0, has_side_effects=True, vmem_limit_bytes=60 * 2**20
        ),
        name="layer",
    )(tokens, pair_row, cotangent, up_table, down_table, up_weight, down_weight)
    return pl.pallas_call(
        settle_kernel,
        out_shape=[jax.ShapeDtypeStruct(tokens.shape, jnp.bfloat16)] * 2,
        in_specs=[vmem] * 2,
        out_specs=[vmem] * 2,
        name="settle",
    )(rows, turned)


def place(pair_ids, groups, capacity):
    target = pair_ids % groups
    matches = (target[:, None] == jnp.arange(groups, dtype=jnp.int32)[None, :]).astype(jnp.int32)
    before = jnp.sum((jnp.cumsum(matches, axis=0) - matches) * matches, axis=1)
    position = target * capacity + before
    slots = jnp.arange(groups * capacity, dtype=jnp.int32)
    return (position[None, :] == slots[:, None]).astype(jnp.bfloat16)


def swap(values, groups, capacity):
    width = values.shape[1]
    moved = lax.all_to_all(
        values.reshape(groups, capacity, width), "dp", split_axis=0, concat_axis=0, tiled=True
    )
    return moved.reshape(groups * capacity, width)


def per_device(tokens, cotangent, pair_ids, up_mask, down_mask, up_weight, down_weight):
    groups = lax.axis_size("dp")
    tok_count, part = tokens.shape
    pairs = up_mask.shape[0]
    capacity = max(2, (3 * tok_count + 2 * groups - 1) // (2 * groups))
    slot_count = groups * capacity
    lanes = -(-pairs // BLOCK) * BLOCK
    pad = ((0, 0), (0, 0), (0, lanes - pairs))
    up_table = jnp.transpose(up_mask, (1, 2, 0))
    down_table = jnp.transpose(down_mask, (1, 2, 0))
    sides = lax.axis_size("tensor")
    if sides == 4 and part % 256 == 0 and capacity * part // 256 % 16 == 0 and capacity % 8 == 0:
        return layer(
            tokens, cotangent, pair_ids.reshape(1, tok_count), up_table, down_table, up_weight,
            down_weight[0], groups, capacity, sides,
        )

    placer = place(pair_ids, groups, capacity)
    known = (pair_ids[:, None] == jnp.arange(lanes, dtype=jnp.int32)[None, :]).astype(jnp.bfloat16)
    leaving = jnp.concatenate([tokens, cotangent, known], axis=1)
    moved = swap(dot(placer, leaving).astype(jnp.bfloat16), groups, capacity)
    both = jnp.stack([moved[:, :part], moved[:, part : 2 * part]])
    whole = lax.all_gather(both, "tensor", axis=2, tiled=True)
    mixed_part, input_part = compute(
        whole[0], whole[1], moved[:, 2 * part :], jnp.pad(up_table, pad), jnp.pad(down_table, pad), up_weight, down_weight[0]
    )
    summed = lax.psum_scatter(
        jnp.stack([mixed_part, input_part]), "tensor", scatter_dimension=2, tiled=True
    )
    back = swap(jnp.concatenate([summed[0], summed[1]], axis=1), groups, capacity)
    out = lax.dot_general(
        placer, back, (((0,), (0,)), ((), ())), preferred_element_type=jnp.float32
    ).astype(jnp.bfloat16)
    return out[:, :part], out[:, part:]


def solution(mesh):
    return jax.shard_map(
        per_device,
        mesh=mesh,
        in_specs=(
            P("dp", "tensor"),
            P("dp", "tensor"),
            P("dp"),
            P(None, None, "tensor"),
            P(None, "tensor", None),
            P(None, "tensor"),
            P("dp", "tensor", None),
        ),
        out_specs=(P("dp", "tensor"), P("dp", "tensor")),
        check_vma=False,
    )
```

```python
import functools

import jax
import jax.numpy as jnp
from jax import lax
from jax.experimental import pallas as pl
from jax.experimental.pallas import tpu as pltpu
from jax.sharding import PartitionSpec as P

BLOCK = 128
ROOT = 0.7978845608028654
CUBE = 0.044715
NT = (((1,), (1,)), ((), ()))
NN = (((1,), (0,)), ((), ()))


def dot(a, b, dims=NN):
    return lax.dot_general(a, b, dims, preferred_element_type=jnp.float32)


def gelu_pair(v):
    square = v * v
    t = jnp.tanh(ROOT * (v + CUBE * v * square))
    half = 0.5 * (1.0 + t)
    slope = half + 0.5 * v * (1.0 - t * t) * (ROOT * (1.0 + 3.0 * CUBE * square))
    return v * half, slope


def masked(values_ref, bits, blocks):
    rows = values_ref.shape[0]
    parts = []
    for b in range(blocks):
        own = jnp.broadcast_to(bits[:, b : b + 1], (rows, BLOCK))
        parts.append(values_ref[:, b * BLOCK : (b + 1) * BLOCK] * own)
    return jnp.concatenate(parts, axis=1)


def products(x_ref, g_ref, pick, up_ref, down_ref, wu_ref, wd_ref, h_ref, q_ref, mixed_ref, input_ref):
    blocks_d, blocks_f = up_ref.shape[0], up_ref.shape[1]

    def first(f, _):
        at = pl.ds(pl.multiple_of(f * BLOCK, BLOCK), BLOCK)
        up_bits = dot(pick, up_ref[:, f, :].astype(jnp.bfloat16), NT).astype(jnp.bfloat16)
        down_bits = dot(pick, down_ref[f].astype(jnp.bfloat16), NT).astype(jnp.bfloat16)
        pre = dot(masked(x_ref, up_bits, blocks_d), wu_ref[:, at])
        grad = dot(masked(g_ref, down_bits, blocks_d), wd_ref[at, :], NT)
        act, slope = gelu_pair(pre)
        h_ref[:, at] = act.astype(jnp.bfloat16)
        q_ref[:, at] = (grad * slope).astype(jnp.bfloat16)
        return 0

    def second(d, _):
        at = pl.ds(pl.multiple_of(d * BLOCK, BLOCK), BLOCK)
        up_bits = dot(pick, up_ref[d].astype(jnp.bfloat16), NT).astype(jnp.bfloat16)
        down_bits = dot(pick, down_ref[:, d, :].astype(jnp.bfloat16), NT).astype(jnp.bfloat16)
        mixed_ref[:, at] = dot(masked(h_ref, down_bits, blocks_f), wd_ref[:, at]).astype(jnp.bfloat16)
        input_ref[:, at] = dot(masked(q_ref, up_bits, blocks_f), wu_ref[at, :], NT).astype(jnp.bfloat16)
        return 0

    lax.fori_loop(0, blocks_f, first, 0)
    lax.fori_loop(0, blocks_d, second, 0)


def compute_kernel(x_ref, g_ref, pick_ref, up_ref, down_ref, wu_hbm, wd_hbm, mixed_ref, input_ref,
                   wu_ref, wd_ref, h_ref, q_ref, sems):
    load_up = pltpu.make_async_copy(wu_hbm, wu_ref, sems.at[0])
    load_down = pltpu.make_async_copy(wd_hbm, wd_ref, sems.at[1])
    load_up.start()
    load_down.start()
    load_up.wait()
    load_down.wait()
    products(x_ref, g_ref, pick_ref[...], up_ref, down_ref, wu_ref, wd_ref, h_ref, q_ref, mixed_ref, input_ref)


def compute(x, g, pick, up_table, down_table, up_weight, down_weight):
    rows, width = x.shape
    hidden = up_weight.shape[1]
    vmem = pl.BlockSpec(memory_space=pltpu.VMEM)
    anywhere = pl.BlockSpec(memory_space=pl.ANY)
    return pl.pallas_call(
        compute_kernel,
        out_shape=[jax.ShapeDtypeStruct((rows, width), jnp.bfloat16)] * 2,
        in_specs=[vmem] * 5 + [anywhere] * 2,
        out_specs=[vmem] * 2,
        scratch_shapes=[
            pltpu.VMEM(up_weight.shape, jnp.bfloat16),
            pltpu.VMEM(down_weight.shape, jnp.bfloat16),
            pltpu.VMEM((rows, hidden), jnp.bfloat16),
            pltpu.VMEM((rows, hidden), jnp.bfloat16),
            pltpu.SemaphoreType.DMA((2,)),
        ],
        compiler_params=pltpu.CompilerParams(vmem_limit_bytes=44 * 2**20),
        name="masked_products",
    )(x, g, pick, up_table, down_table, up_weight, down_weight)


MESH = pl.DeviceIdType.MESH


def stacked(values, row, count):
    wide = values.shape[1] // BLOCK
    return jnp.concatenate(
        [values[row : row + count, b * BLOCK : (b + 1) * BLOCK] for b in range(wide)], axis=0
    ).astype(jnp.bfloat16)


def unstack(slab, into_ref, row, column, count):
    wide = slab.astype(jnp.float32)
    for b in range(slab.shape[0] // count):
        into_ref[row : row + count, column + b * BLOCK : column + (b + 1) * BLOCK] = wide[
            b * count : (b + 1) * count
        ]


def layer_kernel(groups, capacity, tokens_ref, pairs_ref, cotangent_hbm, up_hbm, down_hbm, wu_hbm, wd_hbm,
                 rows_ref, turned_ref,
                 wu_ref, wd_ref, up_ref, down_ref, cotangent_ref, eu_ref, ed_ref,
                 send_p, send_a, send_b, got_p, got_a, got_b,
                 wide_ref, x_ref, g_ref, h_ref, q_ref, slope_ref,
                 part_m, part_i, sib_m, sib_i, out_m, out_i, in_m, in_i,
                 back_m, back_i, home_m, home_i, local_sems, ss, rs):
    slots = groups * capacity
    blocks_d, blocks_f = up_ref.shape[0], up_ref.shape[1]
    tok_count, part = tokens_ref.shape
    chunks, chunk = part_m.shape[0], part_m.shape[3]
    blocks_p, blocks_c = part // BLOCK, chunk // BLOCK
    pair_count = up_ref.shape[2]
    lanes = send_p.shape[2]
    me, t = lax.axis_index("dp"), lax.axis_index("tensor")
    core, x = t % 2, t // 2
    sibling, across = 2 * x + 1 - core, 2 * (1 - x) + core
    others = [(me + k) % groups for k in range(1, groups)]

    load_up = pltpu.make_async_copy(wu_hbm, wu_ref, local_sems.at[0])
    load_down = pltpu.make_async_copy(wd_hbm, wd_ref, local_sems.at[1])
    load_ut = pltpu.make_async_copy(up_hbm, up_ref, local_sems.at[2])
    load_dt = pltpu.make_async_copy(down_hbm, down_ref, local_sems.at[3])
    load_cot = pltpu.make_async_copy(cotangent_hbm, cotangent_ref, local_sems.at[4])
    load_ut.start()
    load_dt.start()
    load_cot.start()
    load_up.start()
    load_down.start()

    barrier = pltpu.get_barrier_semaphore()
    for j in others:
        pl.semaphore_signal(barrier, inc=1, device_id={"dp": j}, device_id_type=MESH)
    for s in (sibling, across):
        pl.semaphore_signal(barrier, inc=1, device_id={"tensor": s}, device_id_type=MESH)

    pairs = pairs_ref[...]
    target = lax.rem(pairs, jnp.full_like(pairs, groups))
    group_of = lax.broadcasted_iota(jnp.int32, (groups, tok_count), 0)
    match = group_of == target
    earlier = (
        lax.broadcasted_iota(jnp.int32, (tok_count, tok_count), 0)
        < lax.broadcasted_iota(jnp.int32, (tok_count, tok_count), 1)
    ).astype(jnp.float32).astype(jnp.bfloat16)
    before = dot(match.astype(jnp.float32).astype(jnp.bfloat16), earlier)
    spot = before + (group_of * capacity).astype(jnp.float32)
    position = jnp.sum(jnp.where(match, spot, 0.0), axis=0, keepdims=True)
    slot_of = lax.broadcasted_iota(jnp.int32, (slots, tok_count), 0).astype(jnp.float32)
    placed = (slot_of == position).astype(jnp.float32)
    placer = placed.astype(jnp.bfloat16)
    turned_ref[...] = placed.T.astype(jnp.bfloat16)
    known = (lax.broadcasted_iota(jnp.int32, (lanes, tok_count), 0) == pairs).astype(jnp.float32)
    moved = dot(placer, known.astype(jnp.bfloat16), NT)
    room = send_p.shape[1] - capacity
    for j in range(groups):
        own = moved[j * capacity : (j + 1) * capacity]
        if room:
            own = jnp.concatenate([own, jnp.zeros((room, lanes), jnp.float32)], axis=0)
        send_p[j] = own.astype(jnp.bfloat16)
    got_p[me] = send_p[me]

    pl.semaphore_wait(barrier, groups + 1)

    def remote(src, dst, sem, where):
        return pltpu.make_async_remote_copy(
            src_ref=src, dst_ref=dst, send_sem=ss.at[sem], recv_sem=rs.at[sem],
            device_id=where, device_id_type=MESH,
        )

    step = groups - 1
    every = []

    def launch(copies):
        for copy in copies:
            copy.start()
        every.extend(copies)
        return copies

    def arrive(copies):
        for copy in copies:
            copy.wait_recv()

    trip_p = launch([
        remote(send_p.at[j], got_p.at[me], k, {"dp": j}) for k, j in enumerate(others)
    ])

    def dispatch(values_ref, send, got, first):
        moved = dot(placer, values_ref[...])
        for j in range(groups):
            send[j] = stacked(moved, j * capacity, capacity)
        got[t, me] = send[me]
        return launch([
            remote(send.at[j], got.at[t, me], first + k, {"dp": j}) for k, j in enumerate(others)
        ])

    trip_a = dispatch(tokens_ref, send_a, got_a, step)
    base = 3 * step

    def share(got, first):
        return launch([
            remote(got.at[t], got.at[t], first, {"tensor": across}),
            remote(got.at[t], got.at[t], first + 1, {"tensor": sibling}),
        ])

    def forward(got, first):
        return launch([remote(got.at[across], got.at[across], first + 2, {"tensor": sibling})])

    arrive(trip_p)
    for i in range(groups):
        unstack(got_p[i, :capacity], wide_ref, i * capacity, 0, capacity)
    pick = wide_ref[:, :pair_count].astype(jnp.bfloat16)
    load_ut.wait()
    load_dt.wait()
    load_cot.wait()

    def expand(table, into_ref, f):
        bits = dot(pick, table.astype(jnp.float32).astype(jnp.bfloat16), NT).astype(jnp.bfloat16)
        for d in range(blocks_d):
            into_ref[f, :, d * BLOCK : (d + 1) * BLOCK] = jnp.broadcast_to(
                bits[:, d : d + 1], (slots, BLOCK)
            )

    def steps(low, high, at_once, one, stride=1):
        def several(n, _):
            for k in range(0, at_once, stride):
                one(low + n * at_once + k)
            return 0

        lax.fori_loop(0, (high - low) // at_once, several, 0)

    half = blocks_f // 2
    steps(0, blocks_f, 2, lambda f: expand(up_ref[:, f, :], eu_ref, f))
    arrive(trip_a)
    share_a = share(got_a, base)
    trip_b = dispatch(cotangent_ref, send_b, got_b, 2 * step)
    steps(0, half, 2, lambda f: expand(down_ref[f], ed_ref, f))
    arrive(share_a[:1])
    forward_a = forward(got_a, base)
    steps(half, blocks_f, 2, lambda f: expand(down_ref[f], ed_ref, f))
    arrive(share_a[1:] + forward_a)

    def assemble(got, into_ref):
        for s in range(got.shape[0]):
            for i in range(groups):
                unstack(got[s, i], wide_ref, i * capacity, s * part, capacity)
        into_ref[...] = wide_ref[...].astype(jnp.bfloat16)

    assemble(got_a, x_ref)
    load_up.wait()

    def columns(b):
        return pl.ds(pl.multiple_of(b * BLOCK, BLOCK), BLOCK)

    def double(b):
        return pl.ds(pl.multiple_of(b * BLOCK, 2 * BLOCK), 2 * BLOCK)

    def quarters(rows_of, weights, dims):
        tall = jnp.concatenate([rows_of(0), rows_of(1)], axis=0)
        square = dot(tall, weights, dims)
        return square[:slots, :BLOCK], square[slots:, BLOCK:]

    def pre_step(f):
        both = quarters(lambda n: x_ref[...] * eu_ref[f + n], wu_ref[:, double(f)], NN)
        for n, pre in enumerate(both):
            act, slope = gelu_pair(pre)
            h_ref[:, columns(f + n)] = act.astype(jnp.bfloat16)
            slope_ref[:, columns(f + n)] = slope

    def grad_step(f):
        both = quarters(lambda n: g_ref[...] * ed_ref[f + n], wd_ref[double(f), :], NT)
        for n, grad in enumerate(both):
            q_ref[:, columns(f + n)] = (grad * slope_ref[:, columns(f + n)]).astype(jnp.bfloat16)

    def picked(values_ref, bits_ref, d):
        return jnp.concatenate(
            [
                values_ref[:, f * BLOCK : (f + 1) * BLOCK] * bits_ref[f, :, columns(d)]
                for f in range(blocks_f)
            ],
            axis=1,
        )

    def mixed_pair(d):
        return quarters(lambda n: picked(h_ref, ed_ref, d + n), wd_ref[:, double(d)], NN)

    def input_pair(d):
        return quarters(lambda n: picked(q_ref, eu_ref, d + n), wu_ref[double(d), :], NT)

    class Sums:
        def __init__(self, block, part_ref, sib_ref, out_ref, in_ref, back_ref, home_ref, first):
            self.block, self.part, self.sib, self.out = block, part_ref, sib_ref, out_ref
            self.into, self.back, self.home, self.first = in_ref, back_ref, home_ref, first

        def to_sibling(self, h, n):
            side = (1 - x, x)[n]
            return remote(
                self.part.at[h, 2 * side + 1 - core], self.sib.at[h, side],
                self.first + h * (3 + step) + n, {"tensor": sibling},
            )

        def to_across(self, h):
            return remote(
                self.out.at[h], self.into.at[h], self.first + h * (3 + step) + 2, {"tensor": across}
            )

        def to_home(self, h):
            return [
                remote(
                    self.back.at[h, j], self.home.at[h, me],
                    self.first + h * (3 + step) + 3 + k, {"dp": j},
                )
                for k, j in enumerate(others)
            ]

        def fill(self, h, owner):
            for b in range(0, blocks_c, 2):
                both = self.block(owner * blocks_p + h * blocks_c + b)
                for n, value in enumerate(both):
                    at = (b + n) * BLOCK
                    self.part[h, owner, :, at : at + BLOCK] = value.astype(jnp.bfloat16)

        def launch_home(self, h):
            self.to_sibling(h, 1).wait_recv()
            self.to_across(h).wait_recv()
            summed = (
                self.part[h, t].astype(jnp.float32)
                + self.sib[h, x].astype(jnp.float32)
                + self.into[h].astype(jnp.float32)
            )
            for i in range(groups):
                self.back[h, i] = stacked(summed, i * capacity, capacity)
            self.home[h, me] = self.back[h, me]
            for copy in self.to_home(h):
                copy.start()

        def run(self, hook):
            def one(h, _):
                self.fill(h, 2 * (1 - x) + 1 - core)
                self.to_sibling(h, 0).start()

                @pl.when(h > 0)
                def _():
                    hook()
                    self.launch_home(h - 1)

                self.fill(h, across)
                self.to_sibling(h, 0).wait_recv()
                self.out[h] = (
                    self.part[h, across].astype(jnp.float32) + self.sib[h, 1 - x].astype(jnp.float32)
                ).astype(jnp.bfloat16)
                self.to_across(h).start()
                self.fill(h, 2 * x + 1 - core)
                self.to_sibling(h, 1).start()
                self.fill(h, t)
                return 0

            lax.fori_loop(0, chunks, one, 0)

        def finish(self, n):
            for h in range(chunks):
                for copy in self.to_home(h):
                    copy.wait_recv()
                for i in range(groups):
                    unstack(self.home[h, i], wide_ref, i * capacity, h * chunk, capacity)
            rows_ref[n] = wide_ref[:, :part].astype(jnp.bfloat16)

        def settle(self):
            for h in range(chunks):
                for copy in [self.to_sibling(h, 0), self.to_sibling(h, 1), self.to_across(h)] + self.to_home(h):
                    copy.wait_send()

    sums_m = Sums(mixed_pair, part_m, sib_m, out_m, in_m, back_m, home_m, base + 6)
    sums_i = Sums(
        input_pair, part_i, sib_i, out_i, in_i, back_i, home_i, base + 6 + chunks * (3 + step)
    )

    steps(0, half, 4, pre_step, 2)
    arrive(trip_b)
    share_b = share(got_b, base + 3)
    steps(half, blocks_f, 4, pre_step, 2)
    load_down.wait()
    forward_b = remote(got_b.at[across], got_b.at[across], base + 5, {"tensor": sibling})

    def pass_on():
        share_b[0].wait_recv()
        forward_b.start()

    sums_m.run(pass_on)
    share_b[1].wait_recv()
    forward_b.wait_recv()
    assemble(got_b, g_ref)
    steps(0, half, 4, grad_step, 2)
    sums_m.launch_home(chunks - 1)
    steps(half, blocks_f, 4, grad_step, 2)
    sums_i.run(lambda: None)
    sums_i.launch_home(chunks - 1)
    sums_m.finish(0)
    sums_i.finish(1)
    for copy in every:
        copy.wait_send()
    forward_b.wait_send()
    sums_m.settle()
    sums_i.settle()


def settle_kernel(rows_ref, turned_ref, mixed_ref, grads_ref):
    turned = turned_ref[...]
    mixed_ref[...] = dot(turned, rows_ref[0]).astype(jnp.bfloat16)
    grads_ref[...] = dot(turned, rows_ref[1]).astype(jnp.bfloat16)


def layer(tokens, cotangent, pair_row, up_table, down_table, up_weight, down_weight, groups, capacity, sides):
    part = tokens.shape[1]
    slots = groups * capacity
    width = part * sides
    hidden = up_weight.shape[1]
    blocks_f = hidden // BLOCK
    lanes = -(-up_table.shape[2] // BLOCK) * BLOCK
    chunks = 2
    chunk = part // chunks
    tall = capacity * part // BLOCK
    short = -(-capacity // 16) * 16
    vmem = pl.BlockSpec(memory_space=pltpu.VMEM)
    anywhere = pl.BlockSpec(memory_space=pl.ANY)
    trips = 3 * (groups - 1) + 6 + 2 * chunks * (groups + 2)

    def buffer(*shape):
        return pltpu.VMEM(shape, jnp.bfloat16)

    rows, turned = pl.pallas_call(
        functools.partial(layer_kernel, groups, capacity),
        out_shape=[
            jax.ShapeDtypeStruct((2, slots, part), jnp.bfloat16),
            jax.ShapeDtypeStruct((tokens.shape[0], slots), jnp.bfloat16),
        ],
        in_specs=[vmem] * 2 + [anywhere] * 5,
        out_specs=[vmem] * 2,
        scratch_shapes=[
            buffer(*up_weight.shape),
            buffer(*down_weight.shape),
            pltpu.VMEM(up_table.shape, jnp.int32),
            pltpu.VMEM(down_table.shape, jnp.int32),
            buffer(*cotangent.shape),
            buffer(blocks_f, slots, width),
            buffer(blocks_f, slots, width),
            buffer(groups, short, lanes),
            buffer(groups, tall, BLOCK),
            buffer(groups, tall, BLOCK),
            buffer(groups, short, lanes),
            buffer(sides, groups, tall, BLOCK),
            buffer(sides, groups, tall, BLOCK),
            pltpu.VMEM((slots, width), jnp.float32),
            buffer(slots, width),
            buffer(slots, width),
            buffer(slots, hidden),
            buffer(slots, hidden),
            pltpu.VMEM((slots, hidden), jnp.float32),
            buffer(chunks, sides, slots, chunk),
            buffer(chunks, sides, slots, chunk),
            buffer(chunks, 2, slots, chunk),
            buffer(chunks, 2, slots, chunk),
            buffer(chunks, slots, chunk),
            buffer(chunks, slots, chunk),
            buffer(chunks, slots, chunk),
            buffer(chunks, slots, chunk),
            buffer(chunks, groups, tall // chunks, BLOCK),
            buffer(chunks, groups, tall // chunks, BLOCK),
            buffer(chunks, groups, tall // chunks, BLOCK),
            buffer(chunks, groups, tall // chunks, BLOCK),
            pltpu.SemaphoreType.DMA((5,)),
            pltpu.SemaphoreType.DMA((trips,)),
            pltpu.SemaphoreType.DMA((trips,)),
        ],
        compiler_params=pltpu.CompilerParams(
            collective_id=0, has_side_effects=True, vmem_limit_bytes=60 * 2**20
        ),
        name="layer",
    )(tokens, pair_row, cotangent, up_table, down_table, up_weight, down_weight)
    return pl.pallas_call(
        settle_kernel,
        out_shape=[jax.ShapeDtypeStruct(tokens.shape, jnp.bfloat16)] * 2,
        in_specs=[vmem] * 2,
        out_specs=[vmem] * 2,
        name="settle",
    )(rows, turned)


def place(pair_ids, groups, capacity):
    target = pair_ids % groups
    matches = (target[:, None] == jnp.arange(groups, dtype=jnp.int32)[None, :]).astype(jnp.int32)
    before = jnp.sum((jnp.cumsum(matches, axis=0) - matches) * matches, axis=1)
    position = target * capacity + before
    slots = jnp.arange(groups * capacity, dtype=jnp.int32)
    return (position[None, :] == slots[:, None]).astype(jnp.bfloat16)


def swap(values, groups, capacity):
    width = values.shape[1]
    moved = lax.all_to_all(
        values.reshape(groups, capacity, width), "dp", split_axis=0, concat_axis=0, tiled=True
    )
    return moved.reshape(groups * capacity, width)


def per_device(tokens, cotangent, pair_ids, up_mask, down_mask, up_weight, down_weight):
    groups = lax.axis_size("dp")
    tok_count, part = tokens.shape
    pairs = up_mask.shape[0]
    capacity = max(2, (3 * tok_count + 2 * groups - 1) // (2 * groups))
    slot_count = groups * capacity
    lanes = -(-pairs // BLOCK) * BLOCK
    pad = ((0, 0), (0, 0), (0, lanes - pairs))
    up_table = jnp.transpose(up_mask, (1, 2, 0))
    down_table = jnp.transpose(down_mask, (1, 2, 0))
    sides = lax.axis_size("tensor")
    if sides == 4 and part % 512 == 0 and up_weight.shape[1] % 1024 == 0 and capacity * part // 256 % 16 == 0 and capacity % 8 == 0:
        return layer(
            tokens, cotangent, pair_ids.reshape(1, tok_count), up_table, down_table, up_weight,
            down_weight[0], groups, capacity, sides,
        )

    placer = place(pair_ids, groups, capacity)
    known = (pair_ids[:, None] == jnp.arange(lanes, dtype=jnp.int32)[None, :]).astype(jnp.bfloat16)
    leaving = jnp.concatenate([tokens, cotangent, known], axis=1)
    moved = swap(dot(placer, leaving).astype(jnp.bfloat16), groups, capacity)
    both = jnp.stack([moved[:, :part], moved[:, part : 2 * part]])
    whole = lax.all_gather(both, "tensor", axis=2, tiled=True)
    mixed_part, input_part = compute(
        whole[0], whole[1], moved[:, 2 * part :], jnp.pad(up_table, pad), jnp.pad(down_table, pad), up_weight, down_weight[0]
    )
    summed = lax.psum_scatter(
        jnp.stack([mixed_part, input_part]), "tensor", scatter_dimension=2, tiled=True
    )
    back = swap(jnp.concatenate([summed[0], summed[1]], axis=1), groups, capacity)
    out = lax.dot_general(
        placer, back, (((0,), (0,)), ((), ())), preferred_element_type=jnp.float32
    ).astype(jnp.bfloat16)
    return out[:, :part], out[:, part:]


def solution(mesh):
    return jax.shard_map(
        per_device,
        mesh=mesh,
        in_specs=(
            P("dp", "tensor"),
            P("dp", "tensor"),
            P("dp"),
            P(None, None, "tensor"),
            P(None, "tensor", None),
            P(None, "tensor"),
            P("dp", "tensor", None),
        ),
        out_specs=(P("dp", "tensor"), P("dp", "tensor")),
        check_vma=False,
    )
```

```python
import functools

import jax
import jax.numpy as jnp
from jax import lax
from jax.experimental import pallas as pl
from jax.experimental.pallas import tpu as pltpu
from jax.sharding import PartitionSpec as P

BLOCK = 128
ROOT = 0.7978845608028654
CUBE = 0.044715
NT = (((1,), (1,)), ((), ()))
NN = (((1,), (0,)), ((), ()))


def dot(a, b, dims=NN):
    return lax.dot_general(a, b, dims, preferred_element_type=jnp.float32)


def gelu_pair(v):
    square = v * v
    t = jnp.tanh(ROOT * (v + CUBE * v * square))
    half = 0.5 * (1.0 + t)
    slope = half + 0.5 * v * (1.0 - t * t) * (ROOT * (1.0 + 3.0 * CUBE * square))
    return v * half, slope


def masked(values_ref, bits, blocks):
    rows = values_ref.shape[0]
    parts = []
    for b in range(blocks):
        own = jnp.broadcast_to(bits[:, b : b + 1], (rows, BLOCK))
        parts.append(values_ref[:, b * BLOCK : (b + 1) * BLOCK] * own)
    return jnp.concatenate(parts, axis=1)


def products(x_ref, g_ref, pick, up_ref, down_ref, wu_ref, wd_ref, h_ref, q_ref, mixed_ref, input_ref):
    blocks_d, blocks_f = up_ref.shape[0], up_ref.shape[1]

    def first(f, _):
        at = pl.ds(pl.multiple_of(f * BLOCK, BLOCK), BLOCK)
        up_bits = dot(pick, up_ref[:, f, :].astype(jnp.bfloat16), NT).astype(jnp.bfloat16)
        down_bits = dot(pick, down_ref[f].astype(jnp.bfloat16), NT).astype(jnp.bfloat16)
        pre = dot(masked(x_ref, up_bits, blocks_d), wu_ref[:, at])
        grad = dot(masked(g_ref, down_bits, blocks_d), wd_ref[at, :], NT)
        act, slope = gelu_pair(pre)
        h_ref[:, at] = act.astype(jnp.bfloat16)
        q_ref[:, at] = (grad * slope).astype(jnp.bfloat16)
        return 0

    def second(d, _):
        at = pl.ds(pl.multiple_of(d * BLOCK, BLOCK), BLOCK)
        up_bits = dot(pick, up_ref[d].astype(jnp.bfloat16), NT).astype(jnp.bfloat16)
        down_bits = dot(pick, down_ref[:, d, :].astype(jnp.bfloat16), NT).astype(jnp.bfloat16)
        mixed_ref[:, at] = dot(masked(h_ref, down_bits, blocks_f), wd_ref[:, at]).astype(jnp.bfloat16)
        input_ref[:, at] = dot(masked(q_ref, up_bits, blocks_f), wu_ref[at, :], NT).astype(jnp.bfloat16)
        return 0

    lax.fori_loop(0, blocks_f, first, 0)
    lax.fori_loop(0, blocks_d, second, 0)


def compute_kernel(x_ref, g_ref, pick_ref, up_ref, down_ref, wu_hbm, wd_hbm, mixed_ref, input_ref,
                   wu_ref, wd_ref, h_ref, q_ref, sems):
    load_up = pltpu.make_async_copy(wu_hbm, wu_ref, sems.at[0])
    load_down = pltpu.make_async_copy(wd_hbm, wd_ref, sems.at[1])
    load_up.start()
    load_down.start()
    load_up.wait()
    load_down.wait()
    products(x_ref, g_ref, pick_ref[...], up_ref, down_ref, wu_ref, wd_ref, h_ref, q_ref, mixed_ref, input_ref)


def compute(x, g, pick, up_table, down_table, up_weight, down_weight):
    rows, width = x.shape
    hidden = up_weight.shape[1]
    vmem = pl.BlockSpec(memory_space=pltpu.VMEM)
    anywhere = pl.BlockSpec(memory_space=pl.ANY)
    return pl.pallas_call(
        compute_kernel,
        out_shape=[jax.ShapeDtypeStruct((rows, width), jnp.bfloat16)] * 2,
        in_specs=[vmem] * 5 + [anywhere] * 2,
        out_specs=[vmem] * 2,
        scratch_shapes=[
            pltpu.VMEM(up_weight.shape, jnp.bfloat16),
            pltpu.VMEM(down_weight.shape, jnp.bfloat16),
            pltpu.VMEM((rows, hidden), jnp.bfloat16),
            pltpu.VMEM((rows, hidden), jnp.bfloat16),
            pltpu.SemaphoreType.DMA((2,)),
        ],
        compiler_params=pltpu.CompilerParams(vmem_limit_bytes=44 * 2**20),
        name="masked_products",
    )(x, g, pick, up_table, down_table, up_weight, down_weight)


MESH = pl.DeviceIdType.MESH


def stacked(values, row, count):
    wide = values.shape[1] // BLOCK
    return jnp.concatenate(
        [values[row : row + count, b * BLOCK : (b + 1) * BLOCK] for b in range(wide)], axis=0
    ).astype(jnp.bfloat16)


def unstack(slab, into_ref, row, column, count):
    wide = slab.astype(jnp.float32)
    for b in range(slab.shape[0] // count):
        into_ref[row : row + count, column + b * BLOCK : column + (b + 1) * BLOCK] = wide[
            b * count : (b + 1) * count
        ]


def layer_kernel(groups, capacity, tokens_ref, pairs_ref, cotangent_hbm, up_hbm, down_hbm, wu_hbm, wd_hbm,
                 rows_ref, turned_ref,
                 wu_ref, wd_ref, up_ref, down_ref, cotangent_ref, eu_ref, ed_ref,
                 send_p, send_a, send_b, got_p, got_a, got_b,
                 wide_ref, x_ref, g_ref, h_ref, q_ref, slope_ref,
                 part_m, part_i, sib_m, sib_i, out_m, out_i, in_m, in_i,
                 back_m, back_i, home_m, home_i, local_sems, ss, rs):
    slots = groups * capacity
    blocks_d, blocks_f = up_ref.shape[0], up_ref.shape[1]
    tok_count, part = tokens_ref.shape
    blocks_p = part // BLOCK
    pair_count = up_ref.shape[2]
    lanes = send_p.shape[2]
    me, t = lax.axis_index("dp"), lax.axis_index("tensor")
    core, x = t % 2, t // 2
    sibling, across = 2 * x + 1 - core, 2 * (1 - x) + core
    others = [(me + k) % groups for k in range(1, groups)]

    load_up = pltpu.make_async_copy(wu_hbm, wu_ref, local_sems.at[0])
    load_down = pltpu.make_async_copy(wd_hbm, wd_ref, local_sems.at[1])
    load_ut = pltpu.make_async_copy(up_hbm, up_ref, local_sems.at[2])
    load_dt = pltpu.make_async_copy(down_hbm, down_ref, local_sems.at[3])
    load_cot = pltpu.make_async_copy(cotangent_hbm, cotangent_ref, local_sems.at[4])
    load_ut.start()
    load_dt.start()
    load_cot.start()
    load_up.start()
    load_down.start()

    barrier = pltpu.get_barrier_semaphore()
    for j in others:
        pl.semaphore_signal(barrier, inc=1, device_id={"dp": j}, device_id_type=MESH)
    for s in (sibling, across):
        pl.semaphore_signal(barrier, inc=1, device_id={"tensor": s}, device_id_type=MESH)

    pairs = pairs_ref[...]
    target = lax.rem(pairs, jnp.full_like(pairs, groups))
    group_of = lax.broadcasted_iota(jnp.int32, (groups, tok_count), 0)
    match = group_of == target
    earlier = (
        lax.broadcasted_iota(jnp.int32, (tok_count, tok_count), 0)
        < lax.broadcasted_iota(jnp.int32, (tok_count, tok_count), 1)
    ).astype(jnp.float32).astype(jnp.bfloat16)
    before = dot(match.astype(jnp.float32).astype(jnp.bfloat16), earlier)
    spot = before + (group_of * capacity).astype(jnp.float32)
    position = jnp.sum(jnp.where(match, spot, 0.0), axis=0, keepdims=True)
    slot_of = lax.broadcasted_iota(jnp.int32, (slots, tok_count), 0).astype(jnp.float32)
    placed = (slot_of == position).astype(jnp.float32)
    placer = placed.astype(jnp.bfloat16)
    turned_ref[...] = placed.T.astype(jnp.bfloat16)
    known = (lax.broadcasted_iota(jnp.int32, (lanes, tok_count), 0) == pairs).astype(jnp.float32)
    moved = dot(placer, known.astype(jnp.bfloat16), NT)
    room = send_p.shape[1] - capacity
    for j in range(groups):
        own = moved[j * capacity : (j + 1) * capacity]
        if room:
            own = jnp.concatenate([own, jnp.zeros((room, lanes), jnp.float32)], axis=0)
        send_p[j] = own.astype(jnp.bfloat16)
    got_p[me] = send_p[me]

    def pack(values_ref, send, got):
        moved = dot(placer, values_ref[...])
        for j in range(groups):
            send[j] = stacked(moved, j * capacity, capacity)
        got[t, me] = send[me]

    pack(tokens_ref, send_a, got_a)
    pl.semaphore_wait(barrier, groups + 1)

    def remote(src, dst, sem, where):
        return pltpu.make_async_remote_copy(
            src_ref=src, dst_ref=dst, send_sem=ss.at[sem], recv_sem=rs.at[sem],
            device_id=where, device_id_type=MESH,
        )

    step = groups - 1
    every = []

    def launch(copies):
        for copy in copies:
            copy.start()
        every.extend(copies)
        return copies

    def arrive(copies):
        for copy in copies:
            copy.wait_recv()

    trip_p = launch([
        remote(send_p.at[j], got_p.at[me], k, {"dp": j}) for k, j in enumerate(others)
    ])

    def dispatch(send, got, first):
        return launch([
            remote(send.at[j], got.at[t, me], first + k, {"dp": j}) for k, j in enumerate(others)
        ])

    trip_a = dispatch(send_a, got_a, step)
    base = 3 * step

    def share(got, first):
        return launch([
            remote(got.at[t], got.at[t], first, {"tensor": across}),
            remote(got.at[t], got.at[t], first + 1, {"tensor": sibling}),
        ])

    def forward(got, first):
        return launch([remote(got.at[across], got.at[across], first + 2, {"tensor": sibling})])

    arrive(trip_p)
    for i in range(groups):
        unstack(got_p[i, :capacity], wide_ref, i * capacity, 0, capacity)
    pick = wide_ref[:, :pair_count].astype(jnp.bfloat16)
    load_ut.wait()
    load_dt.wait()
    load_cot.wait()

    def expand(table, into_ref, f):
        bits = dot(pick, table.astype(jnp.float32).astype(jnp.bfloat16), NT).astype(jnp.bfloat16)
        for d in range(blocks_d):
            into_ref[f, :, d * BLOCK : (d + 1) * BLOCK] = jnp.broadcast_to(
                bits[:, d : d + 1], (slots, BLOCK)
            )

    def steps(low, high, at_once, one, stride=1):
        def several(n, _):
            for k in range(0, at_once, stride):
                one(low + n * at_once + k)
            return 0

        lax.fori_loop(0, (high - low) // at_once, several, 0)

    half = blocks_f // 2
    steps(0, blocks_f, 2, lambda f: expand(up_ref[:, f, :], eu_ref, f))
    pack(cotangent_ref, send_b, got_b)
    arrive(trip_a)
    share_a = share(got_a, base)
    trip_b = dispatch(send_b, got_b, 2 * step)
    steps(0, half, 2, lambda f: expand(down_ref[f], ed_ref, f))
    arrive(share_a[:1])
    forward_a = forward(got_a, base)
    arrive(share_a[1:] + forward_a)

    def assemble(got, into_ref):
        for s in range(got.shape[0]):
            for i in range(groups):
                unstack(got[s, i], wide_ref, i * capacity, s * part, capacity)
        into_ref[...] = wide_ref[...].astype(jnp.bfloat16)

    assemble(got_a, x_ref)
    load_up.wait()

    def columns(b):
        return pl.ds(pl.multiple_of(b * BLOCK, BLOCK), BLOCK)

    def pre_step(f):
        pre = dot(x_ref[...] * eu_ref[f], wu_ref[:, columns(f)])
        act, slope = gelu_pair(pre)
        h_ref[:, columns(f)] = act.astype(jnp.bfloat16)
        slope_ref[:, columns(f)] = slope

    def pre_pair(f):
        expand(down_ref[half + f // 2], ed_ref, half + f // 2)
        pre_step(f)
        pre_step(f + 1)

    def grad_step(f):
        grad = dot(g_ref[...] * ed_ref[f], wd_ref[columns(f), :], NT)
        q_ref[:, columns(f)] = (grad * slope_ref[:, columns(f)]).astype(jnp.bfloat16)

    def picked(values_ref, bits_ref, d):
        return jnp.concatenate(
            [
                values_ref[:, f * BLOCK : (f + 1) * BLOCK] * bits_ref[f, :, columns(d)]
                for f in range(blocks_f)
            ],
            axis=1,
        )

    def mixed_block(d):
        return dot(picked(h_ref, ed_ref, d), wd_ref[:, columns(d)])

    def input_block(d):
        return dot(picked(q_ref, eu_ref, d), wu_ref[columns(d), :], NT)

    class Sums:
        def __init__(self, block, part_ref, sib_ref, out_ref, in_ref, back_ref, home_ref, first):
            self.block, self.part, self.sib, self.out = block, part_ref, sib_ref, out_ref
            self.into, self.back, self.home, self.first = in_ref, back_ref, home_ref, first
            self.chunks, self.chunk = part_ref.shape[0], part_ref.shape[3]
            self.blocks = self.chunk // BLOCK

        def to_sibling(self, h, n):
            side = (1 - x, x)[n]
            return remote(
                self.part.at[h, 2 * side + 1 - core], self.sib.at[h, side],
                self.first + h * (3 + step) + n, {"tensor": sibling},
            )

        def to_across(self, h):
            return remote(
                self.out.at[h], self.into.at[h], self.first + h * (3 + step) + 2, {"tensor": across}
            )

        def to_home(self, h):
            return [
                remote(
                    self.back.at[h, j], self.home.at[h, me],
                    self.first + h * (3 + step) + 3 + k, {"dp": j},
                )
                for k, j in enumerate(others)
            ]

        def fill(self, h, owner):
            for b in range(self.blocks):
                d = owner * blocks_p + h * self.blocks + b
                self.part[h, owner, :, b * BLOCK : (b + 1) * BLOCK] = self.block(d).astype(jnp.bfloat16)

        def launch_home(self, h):
            self.to_sibling(h, 1).wait_recv()
            self.to_across(h).wait_recv()
            summed = (
                self.part[h, t].astype(jnp.float32)
                + self.sib[h, x].astype(jnp.float32)
                + self.into[h].astype(jnp.float32)
            )
            for i in range(groups):
                self.back[h, i] = stacked(summed, i * capacity, capacity)
            self.home[h, me] = self.back[h, me]
            for copy in self.to_home(h):
                copy.start()

        def run(self, hook):
            def one(h, _):
                self.fill(h, 2 * (1 - x) + 1 - core)
                self.to_sibling(h, 0).start()

                if self.chunks > 1:
                    pl.when(h > 0)(lambda: self.launch_home(h - 1))

                self.fill(h, across)
                self.to_sibling(h, 0).wait_recv()
                self.out[h] = (
                    self.part[h, across].astype(jnp.float32) + self.sib[h, 1 - x].astype(jnp.float32)
                ).astype(jnp.bfloat16)
                self.to_across(h).start()
                hook()
                self.fill(h, 2 * x + 1 - core)
                self.to_sibling(h, 1).start()
                self.fill(h, t)
                return 0

            lax.fori_loop(0, self.chunks, one, 0)

        def finish(self, n):
            for h in range(self.chunks):
                for copy in self.to_home(h):
                    copy.wait_recv()
                for i in range(groups):
                    unstack(self.home[h, i], wide_ref, i * capacity, h * self.chunk, capacity)
            rows_ref[n] = wide_ref[:, :part].astype(jnp.bfloat16)

        def settle(self):
            for h in range(self.chunks):
                for copy in [self.to_sibling(h, 0), self.to_sibling(h, 1), self.to_across(h)] + self.to_home(h):
                    copy.wait_send()

    sums_m = Sums(mixed_block, part_m, sib_m, out_m, in_m, back_m, home_m, base + 6)
    sums_i = Sums(
        input_block, part_i, sib_i, out_i, in_i, back_i, home_i, base + 6 + part_m.shape[0] * (3 + step)
    )

    steps(0, half, 4, pre_pair, 2)
    arrive(trip_b)
    share_b = share(got_b, base + 3)
    steps(half, blocks_f, 4, pre_pair, 2)
    load_down.wait()
    forward_b = remote(got_b.at[across], got_b.at[across], base + 5, {"tensor": sibling})

    def pass_on():
        share_b[0].wait_recv()
        forward_b.start()

    sums_m.run(pass_on)
    share_b[1].wait_recv()
    forward_b.wait_recv()
    assemble(got_b, g_ref)
    steps(0, half, 4, grad_step)
    sums_m.launch_home(sums_m.chunks - 1)
    steps(half, blocks_f, 4, grad_step)
    sums_i.run(lambda: None)
    sums_i.launch_home(sums_i.chunks - 1)
    sums_m.finish(0)
    for copy in every:
        copy.wait_send()
    forward_b.wait_send()
    sums_m.settle()
    sums_i.finish(1)
    sums_i.settle()


def settle_kernel(rows_ref, turned_ref, mixed_ref, grads_ref):
    turned = turned_ref[...]
    mixed_ref[...] = dot(turned, rows_ref[0]).astype(jnp.bfloat16)
    grads_ref[...] = dot(turned, rows_ref[1]).astype(jnp.bfloat16)


def layer(tokens, cotangent, pair_row, up_table, down_table, up_weight, down_weight, groups, capacity, sides):
    part = tokens.shape[1]
    slots = groups * capacity
    width = part * sides
    hidden = up_weight.shape[1]
    blocks_f = hidden // BLOCK
    lanes = -(-up_table.shape[2] // BLOCK) * BLOCK
    chunks = (1, 2)
    tall = capacity * part // BLOCK
    short = -(-capacity // 16) * 16
    vmem = pl.BlockSpec(memory_space=pltpu.VMEM)
    anywhere = pl.BlockSpec(memory_space=pl.ANY)
    trips = 3 * (groups - 1) + 6 + sum(chunks) * (groups + 2)

    def buffer(*shape):
        return pltpu.VMEM(shape, jnp.bfloat16)

    rows, turned = pl.pallas_call(
        functools.partial(layer_kernel, groups, capacity),
        out_shape=[
            jax.ShapeDtypeStruct((2, slots, part), jnp.bfloat16),
            jax.ShapeDtypeStruct((tokens.shape[0], slots), jnp.bfloat16),
        ],
        in_specs=[vmem] * 2 + [anywhere] * 5,
        out_specs=[vmem] * 2,
        scratch_shapes=[
            buffer(*up_weight.shape),
            buffer(*down_weight.shape),
            pltpu.VMEM(up_table.shape, jnp.int32),
            pltpu.VMEM(down_table.shape, jnp.int32),
            buffer(*cotangent.shape),
            buffer(blocks_f, slots, width),
            buffer(blocks_f, slots, width),
            buffer(groups, short, lanes),
            buffer(groups, tall, BLOCK),
            buffer(groups, tall, BLOCK),
            buffer(groups, short, lanes),
            buffer(sides, groups, tall, BLOCK),
            buffer(sides, groups, tall, BLOCK),
            pltpu.VMEM((slots, width), jnp.float32),
            buffer(slots, width),
            buffer(slots, width),
            buffer(slots, hidden),
            buffer(slots, hidden),
            pltpu.VMEM((slots, hidden), jnp.float32),
            *[buffer(n, sides, slots, part // n) for n in chunks],
            *[buffer(n, 2, slots, part // n) for n in chunks],
            *[buffer(n, slots, part // n) for n in chunks * 2],
            *[buffer(n, groups, tall // n, BLOCK) for n in chunks * 2],
            pltpu.SemaphoreType.DMA((5,)),
            pltpu.SemaphoreType.DMA((trips,)),
            pltpu.SemaphoreType.DMA((trips,)),
        ],
        compiler_params=pltpu.CompilerParams(
            collective_id=0, has_side_effects=True, vmem_limit_bytes=60 * 2**20
        ),
        name="layer",
    )(tokens, pair_row, cotangent, up_table, down_table, up_weight, down_weight)
    return pl.pallas_call(
        settle_kernel,
        out_shape=[jax.ShapeDtypeStruct(tokens.shape, jnp.bfloat16)] * 2,
        in_specs=[vmem] * 2,
        out_specs=[vmem] * 2,
        name="settle",
    )(rows, turned)


def place(pair_ids, groups, capacity):
    target = pair_ids % groups
    matches = (target[:, None] == jnp.arange(groups, dtype=jnp.int32)[None, :]).astype(jnp.int32)
    before = jnp.sum((jnp.cumsum(matches, axis=0) - matches) * matches, axis=1)
    position = target * capacity + before
    slots = jnp.arange(groups * capacity, dtype=jnp.int32)
    return (position[None, :] == slots[:, None]).astype(jnp.bfloat16)


def swap(values, groups, capacity):
    width = values.shape[1]
    moved = lax.all_to_all(
        values.reshape(groups, capacity, width), "dp", split_axis=0, concat_axis=0, tiled=True
    )
    return moved.reshape(groups * capacity, width)


def per_device(tokens, cotangent, pair_ids, up_mask, down_mask, up_weight, down_weight):
    groups = lax.axis_size("dp")
    tok_count, part = tokens.shape
    pairs = up_mask.shape[0]
    capacity = max(2, (3 * tok_count + 2 * groups - 1) // (2 * groups))
    slot_count = groups * capacity
    lanes = -(-pairs // BLOCK) * BLOCK
    pad = ((0, 0), (0, 0), (0, lanes - pairs))
    up_table = jnp.transpose(up_mask, (1, 2, 0))
    down_table = jnp.transpose(down_mask, (1, 2, 0))
    sides = lax.axis_size("tensor")
    if sides == 4 and part % 256 == 0 and up_weight.shape[1] % 1024 == 0 and capacity * part // 256 % 16 == 0 and capacity % 8 == 0:
        return layer(
            tokens, cotangent, pair_ids.reshape(1, tok_count), up_table, down_table, up_weight,
            down_weight[0], groups, capacity, sides,
        )

    placer = place(pair_ids, groups, capacity)
    known = (pair_ids[:, None] == jnp.arange(lanes, dtype=jnp.int32)[None, :]).astype(jnp.bfloat16)
    leaving = jnp.concatenate([tokens, cotangent, known], axis=1)
    moved = swap(dot(placer, leaving).astype(jnp.bfloat16), groups, capacity)
    both = jnp.stack([moved[:, :part], moved[:, part : 2 * part]])
    whole = lax.all_gather(both, "tensor", axis=2, tiled=True)
    mixed_part, input_part = compute(
        whole[0], whole[1], moved[:, 2 * part :], jnp.pad(up_table, pad), jnp.pad(down_table, pad), up_weight, down_weight[0]
    )
    summed = lax.psum_scatter(
        jnp.stack([mixed_part, input_part]), "tensor", scatter_dimension=2, tiled=True
    )
    back = swap(jnp.concatenate([summed[0], summed[1]], axis=1), groups, capacity)
    out = lax.dot_general(
        placer, back, (((0,), (0,)), ((), ())), preferred_element_type=jnp.float32
    ).astype(jnp.bfloat16)
    return out[:, :part], out[:, part:]


def solution(mesh):
    return jax.shard_map(
        per_device,
        mesh=mesh,
        in_specs=(
            P("dp", "tensor"),
            P("dp", "tensor"),
            P("dp"),
            P(None, None, "tensor"),
            P(None, "tensor", None),
            P(None, "tensor"),
            P("dp", "tensor", None),
        ),
        out_specs=(P("dp", "tensor"), P("dp", "tensor")),
        check_vma=False,
    )
```

```python
import functools

import jax
import jax.numpy as jnp
from jax import lax
from jax.experimental import pallas as pl
from jax.experimental.pallas import tpu as pltpu
from jax.sharding import PartitionSpec as P

BLOCK = 128
ROOT = 0.7978845608028654
CUBE = 0.044715
NT = (((1,), (1,)), ((), ()))
NN = (((1,), (0,)), ((), ()))


def dot(a, b, dims=NN):
    return lax.dot_general(a, b, dims, preferred_element_type=jnp.float32)


def gelu_pair(v):
    square = v * v
    t = jnp.tanh(ROOT * (v + CUBE * v * square))
    half = 0.5 * (1.0 + t)
    slope = half + 0.5 * v * (1.0 - t * t) * (ROOT * (1.0 + 3.0 * CUBE * square))
    return v * half, slope


def masked(values_ref, bits, blocks):
    rows = values_ref.shape[0]
    parts = []
    for b in range(blocks):
        own = jnp.broadcast_to(bits[:, b : b + 1], (rows, BLOCK))
        parts.append(values_ref[:, b * BLOCK : (b + 1) * BLOCK] * own)
    return jnp.concatenate(parts, axis=1)


def products(x_ref, g_ref, pick, up_ref, down_ref, wu_ref, wd_ref, h_ref, q_ref, mixed_ref, input_ref):
    blocks_d, blocks_f = up_ref.shape[0], up_ref.shape[1]

    def first(f, _):
        at = pl.ds(pl.multiple_of(f * BLOCK, BLOCK), BLOCK)
        up_bits = dot(pick, up_ref[:, f, :].astype(jnp.bfloat16), NT).astype(jnp.bfloat16)
        down_bits = dot(pick, down_ref[f].astype(jnp.bfloat16), NT).astype(jnp.bfloat16)
        pre = dot(masked(x_ref, up_bits, blocks_d), wu_ref[:, at])
        grad = dot(masked(g_ref, down_bits, blocks_d), wd_ref[at, :], NT)
        act, slope = gelu_pair(pre)
        h_ref[:, at] = act.astype(jnp.bfloat16)
        q_ref[:, at] = (grad * slope).astype(jnp.bfloat16)
        return 0

    def second(d, _):
        at = pl.ds(pl.multiple_of(d * BLOCK, BLOCK), BLOCK)
        up_bits = dot(pick, up_ref[d].astype(jnp.bfloat16), NT).astype(jnp.bfloat16)
        down_bits = dot(pick, down_ref[:, d, :].astype(jnp.bfloat16), NT).astype(jnp.bfloat16)
        mixed_ref[:, at] = dot(masked(h_ref, down_bits, blocks_f), wd_ref[:, at]).astype(jnp.bfloat16)
        input_ref[:, at] = dot(masked(q_ref, up_bits, blocks_f), wu_ref[at, :], NT).astype(jnp.bfloat16)
        return 0

    lax.fori_loop(0, blocks_f, first, 0)
    lax.fori_loop(0, blocks_d, second, 0)


def compute_kernel(x_ref, g_ref, pick_ref, up_ref, down_ref, wu_hbm, wd_hbm, mixed_ref, input_ref,
                   wu_ref, wd_ref, h_ref, q_ref, sems):
    load_up = pltpu.make_async_copy(wu_hbm, wu_ref, sems.at[0])
    load_down = pltpu.make_async_copy(wd_hbm, wd_ref, sems.at[1])
    load_up.start()
    load_down.start()
    load_up.wait()
    load_down.wait()
    products(x_ref, g_ref, pick_ref[...], up_ref, down_ref, wu_ref, wd_ref, h_ref, q_ref, mixed_ref, input_ref)


def compute(x, g, pick, up_table, down_table, up_weight, down_weight):
    rows, width = x.shape
    hidden = up_weight.shape[1]
    vmem = pl.BlockSpec(memory_space=pltpu.VMEM)
    anywhere = pl.BlockSpec(memory_space=pl.ANY)
    return pl.pallas_call(
        compute_kernel,
        out_shape=[jax.ShapeDtypeStruct((rows, width), jnp.bfloat16)] * 2,
        in_specs=[vmem] * 5 + [anywhere] * 2,
        out_specs=[vmem] * 2,
        scratch_shapes=[
            pltpu.VMEM(up_weight.shape, jnp.bfloat16),
            pltpu.VMEM(down_weight.shape, jnp.bfloat16),
            pltpu.VMEM((rows, hidden), jnp.bfloat16),
            pltpu.VMEM((rows, hidden), jnp.bfloat16),
            pltpu.SemaphoreType.DMA((2,)),
        ],
        compiler_params=pltpu.CompilerParams(vmem_limit_bytes=44 * 2**20),
        name="masked_products",
    )(x, g, pick, up_table, down_table, up_weight, down_weight)


MESH = pl.DeviceIdType.MESH


def stacked(values, row, count):
    wide = values.shape[1] // BLOCK
    return jnp.concatenate(
        [values[row : row + count, b * BLOCK : (b + 1) * BLOCK] for b in range(wide)], axis=0
    ).astype(jnp.bfloat16)


def unstack(slab, into_ref, row, column, count):
    wide = slab.astype(jnp.float32)
    for b in range(slab.shape[0] // count):
        into_ref[row : row + count, column + b * BLOCK : column + (b + 1) * BLOCK] = wide[
            b * count : (b + 1) * count
        ]


def layer_kernel(groups, capacity, tokens_ref, pairs_ref, cotangent_hbm, up_hbm, down_hbm, wu_hbm, wd_hbm,
                 rows_ref, turned_ref,
                 wu_ref, wd_ref, up_ref, down_ref, cotangent_ref, eu_ref, ed_ref,
                 send_p, send_a, send_b, got_p, got_a, got_b,
                 wide_ref, x_ref, g_ref, h_ref, q_ref, slope_ref,
                 part_m, part_i, sib_m, sib_i, out_m, out_i, in_m, in_i,
                 back_m, back_i, home_m, home_i, local_sems, ss, rs):
    slots = groups * capacity
    blocks_d, blocks_f = up_ref.shape[0], up_ref.shape[1]
    tok_count, part = tokens_ref.shape
    blocks_p = part // BLOCK
    pair_count = up_ref.shape[2]
    lanes = send_p.shape[2]
    me, t = lax.axis_index("dp"), lax.axis_index("tensor")
    core, x = t % 2, t // 2
    sibling, across = 2 * x + 1 - core, 2 * (1 - x) + core
    others = [(me + k) % groups for k in range(1, groups)]

    load_up = pltpu.make_async_copy(wu_hbm, wu_ref, local_sems.at[0])
    load_down = pltpu.make_async_copy(wd_hbm, wd_ref, local_sems.at[1])
    load_ut = pltpu.make_async_copy(up_hbm, up_ref, local_sems.at[2])
    load_dt = pltpu.make_async_copy(down_hbm, down_ref, local_sems.at[3])
    load_cot = pltpu.make_async_copy(cotangent_hbm, cotangent_ref, local_sems.at[4])
    load_ut.start()
    load_dt.start()
    load_cot.start()
    load_up.start()
    load_down.start()

    barrier = pltpu.get_barrier_semaphore()
    for j in others:
        pl.semaphore_signal(barrier, inc=1, device_id={"dp": j}, device_id_type=MESH)
    for s in (sibling, across):
        pl.semaphore_signal(barrier, inc=1, device_id={"tensor": s}, device_id_type=MESH)

    pairs = pairs_ref[...]
    target = lax.rem(pairs, jnp.full_like(pairs, groups))
    group_of = lax.broadcasted_iota(jnp.int32, (groups, tok_count), 0)
    match = group_of == target
    earlier = (
        lax.broadcasted_iota(jnp.int32, (tok_count, tok_count), 0)
        < lax.broadcasted_iota(jnp.int32, (tok_count, tok_count), 1)
    ).astype(jnp.float32).astype(jnp.bfloat16)
    before = dot(match.astype(jnp.float32).astype(jnp.bfloat16), earlier)
    spot = before + (group_of * capacity).astype(jnp.float32)
    position = jnp.sum(jnp.where(match, spot, 0.0), axis=0, keepdims=True)
    slot_of = lax.broadcasted_iota(jnp.int32, (slots, tok_count), 0).astype(jnp.float32)
    placed = (slot_of == position).astype(jnp.float32)
    placer = placed.astype(jnp.bfloat16)
    turned_ref[...] = placed.T.astype(jnp.bfloat16)
    known = (lax.broadcasted_iota(jnp.int32, (lanes, tok_count), 0) == pairs).astype(jnp.float32)
    moved = dot(placer, known.astype(jnp.bfloat16), NT)
    room = send_p.shape[1] - capacity
    for j in range(groups):
        own = moved[j * capacity : (j + 1) * capacity]
        if room:
            own = jnp.concatenate([own, jnp.zeros((room, lanes), jnp.float32)], axis=0)
        send_p[j] = own.astype(jnp.bfloat16)
    got_p[me] = send_p[me]

    def pack(values_ref, send, got):
        moved = dot(placer, values_ref[...])
        for j in range(groups):
            send[j] = stacked(moved, j * capacity, capacity)
        got[t, me] = send[me]

    pack(tokens_ref, send_a, got_a)
    pl.semaphore_wait(barrier, groups + 1)

    def remote(src, dst, sem, where):
        return pltpu.make_async_remote_copy(
            src_ref=src, dst_ref=dst, send_sem=ss.at[sem], recv_sem=rs.at[sem],
            device_id=where, device_id_type=MESH,
        )

    step = groups - 1
    every = []

    def launch(copies):
        for copy in copies:
            copy.start()
        every.extend(copies)
        return copies

    def arrive(copies):
        for copy in copies:
            copy.wait_recv()

    trip_p = launch([
        remote(send_p.at[j], got_p.at[me], k, {"dp": j}) for k, j in enumerate(others)
    ])

    def dispatch(send, got, first):
        return launch([
            remote(send.at[j], got.at[t, me], first + k, {"dp": j}) for k, j in enumerate(others)
        ])

    trip_a = dispatch(send_a, got_a, step)
    base = 3 * step

    def share(got, first):
        return launch([
            remote(got.at[t], got.at[t], first, {"tensor": across}),
            remote(got.at[t], got.at[t], first + 1, {"tensor": sibling}),
        ])

    def forward(got, first):
        return launch([remote(got.at[across], got.at[across], first + 2, {"tensor": sibling})])

    arrive(trip_p)
    for i in range(groups):
        unstack(got_p[i, :capacity], wide_ref, i * capacity, 0, capacity)
    pick = wide_ref[:, :pair_count].astype(jnp.bfloat16)
    load_ut.wait()
    load_dt.wait()
    load_cot.wait()

    def expand(table, into_ref, f):
        bits = dot(pick, table.astype(jnp.float32).astype(jnp.bfloat16), NT).astype(jnp.bfloat16)
        for d in range(blocks_d):
            into_ref[f, :, d * BLOCK : (d + 1) * BLOCK] = jnp.broadcast_to(
                bits[:, d : d + 1], (slots, BLOCK)
            )

    def steps(low, high, at_once, one, stride=1):
        def several(n, _):
            for k in range(0, at_once, stride):
                one(low + n * at_once + k)
            return 0

        lax.fori_loop(0, (high - low) // at_once, several, 0)

    half = blocks_f // 2
    steps(0, blocks_f, 2, lambda f: expand(up_ref[:, f, :], eu_ref, f))
    pack(cotangent_ref, send_b, got_b)
    arrive(trip_a)
    share_a = share(got_a, base)
    trip_b = dispatch(send_b, got_b, 2 * step)
    arrive(share_a[:1])
    forward_a = forward(got_a, base)
    arrive(share_a[1:] + forward_a)

    def assemble(got, into_ref):
        for s in range(got.shape[0]):
            for i in range(groups):
                unstack(got[s, i], wide_ref, i * capacity, s * part, capacity)
        into_ref[...] = wide_ref[...].astype(jnp.bfloat16)

    assemble(got_a, x_ref)
    load_up.wait()

    def columns(b):
        return pl.ds(pl.multiple_of(b * BLOCK, BLOCK), BLOCK)

    def pre_step(f):
        pre = dot(x_ref[...] * eu_ref[f], wu_ref[:, columns(f)])
        act, slope = gelu_pair(pre)
        h_ref[:, columns(f)] = act.astype(jnp.bfloat16)
        slope_ref[:, columns(f)] = slope

    def pre_pair(f):
        for n in range(2):
            expand(down_ref[f + n], ed_ref, f + n)
            pre_step(f + n)

    def grad_step(f):
        grad = dot(g_ref[...] * ed_ref[f], wd_ref[columns(f), :], NT)
        q_ref[:, columns(f)] = (grad * slope_ref[:, columns(f)]).astype(jnp.bfloat16)

    def picked(values_ref, bits_ref, d):
        return jnp.concatenate(
            [
                values_ref[:, f * BLOCK : (f + 1) * BLOCK] * bits_ref[f, :, columns(d)]
                for f in range(blocks_f)
            ],
            axis=1,
        )

    def mixed_block(d):
        return dot(picked(h_ref, ed_ref, d), wd_ref[:, columns(d)])

    def input_block(d):
        return dot(picked(q_ref, eu_ref, d), wu_ref[columns(d), :], NT)

    class Sums:
        def __init__(self, block, part_ref, sib_ref, out_ref, in_ref, back_ref, home_ref, first):
            self.block, self.part, self.sib, self.out = block, part_ref, sib_ref, out_ref
            self.into, self.back, self.home, self.first = in_ref, back_ref, home_ref, first
            self.chunks, self.chunk = part_ref.shape[0], part_ref.shape[3]
            self.blocks = self.chunk // BLOCK

        def to_sibling(self, h, n):
            side = (1 - x, x)[n]
            return remote(
                self.part.at[h, 2 * side + 1 - core], self.sib.at[h, side],
                self.first + h * (3 + step) + n, {"tensor": sibling},
            )

        def to_across(self, h):
            return remote(
                self.out.at[h], self.into.at[h], self.first + h * (3 + step) + 2, {"tensor": across}
            )

        def to_home(self, h):
            return [
                remote(
                    self.back.at[h, j], self.home.at[h, me],
                    self.first + h * (3 + step) + 3 + k, {"dp": j},
                )
                for k, j in enumerate(others)
            ]

        def fill(self, h, owner):
            for b in range(self.blocks):
                d = owner * blocks_p + h * self.blocks + b
                self.part[h, owner, :, b * BLOCK : (b + 1) * BLOCK] = self.block(d).astype(jnp.bfloat16)

        def launch_home(self, h):
            self.to_sibling(h, 1).wait_recv()
            self.to_across(h).wait_recv()
            summed = (
                self.part[h, t].astype(jnp.float32)
                + self.sib[h, x].astype(jnp.float32)
                + self.into[h].astype(jnp.float32)
            )
            for i in range(groups):
                self.back[h, i] = stacked(summed, i * capacity, capacity)
            self.home[h, me] = self.back[h, me]
            for copy in self.to_home(h):
                copy.start()

        def run(self, hook):
            def one(h, _):
                self.fill(h, 2 * (1 - x) + 1 - core)
                self.to_sibling(h, 0).start()

                if self.chunks > 1:
                    pl.when(h > 0)(lambda: self.launch_home(h - 1))

                self.fill(h, across)
                self.to_sibling(h, 0).wait_recv()
                self.out[h] = (
                    self.part[h, across].astype(jnp.float32) + self.sib[h, 1 - x].astype(jnp.float32)
                ).astype(jnp.bfloat16)
                self.to_across(h).start()
                hook()
                self.fill(h, 2 * x + 1 - core)
                self.to_sibling(h, 1).start()
                self.fill(h, t)
                return 0

            lax.fori_loop(0, self.chunks, one, 0)

        def finish(self, n):
            for h in range(self.chunks):
                for copy in self.to_home(h):
                    copy.wait_recv()
                for i in range(groups):
                    unstack(self.home[h, i], wide_ref, i * capacity, h * self.chunk, capacity)
            rows_ref[n] = wide_ref[:, :part].astype(jnp.bfloat16)

        def settle(self):
            for h in range(self.chunks):
                for copy in [self.to_sibling(h, 0), self.to_sibling(h, 1), self.to_across(h)] + self.to_home(h):
                    copy.wait_send()

    sums_m = Sums(mixed_block, part_m, sib_m, out_m, in_m, back_m, home_m, base + 6)
    sums_i = Sums(
        input_block, part_i, sib_i, out_i, in_i, back_i, home_i, base + 6 + part_m.shape[0] * (3 + step)
    )

    steps(0, half, 4, pre_pair, 2)
    arrive(trip_b)
    share_b = share(got_b, base + 3)
    steps(half, blocks_f, 4, pre_pair, 2)
    load_down.wait()
    forward_b = remote(got_b.at[across], got_b.at[across], base + 5, {"tensor": sibling})

    def pass_on():
        share_b[0].wait_recv()
        forward_b.start()

    sums_m.run(pass_on)
    share_b[1].wait_recv()
    forward_b.wait_recv()
    assemble(got_b, g_ref)
    steps(0, half, 4, grad_step)
    sums_m.launch_home(sums_m.chunks - 1)
    steps(half, blocks_f, 4, grad_step)
    sums_i.run(lambda: None)
    sums_i.launch_home(sums_i.chunks - 1)
    sums_m.finish(0)
    for copy in every:
        copy.wait_send()
    forward_b.wait_send()
    sums_m.settle()
    sums_i.finish(1)
    sums_i.settle()


def settle_kernel(rows_ref, turned_ref, mixed_ref, grads_ref):
    turned = turned_ref[...]
    mixed_ref[...] = dot(turned, rows_ref[0]).astype(jnp.bfloat16)
    grads_ref[...] = dot(turned, rows_ref[1]).astype(jnp.bfloat16)


def layer(tokens, cotangent, pair_row, up_table, down_table, up_weight, down_weight, groups, capacity, sides):
    part = tokens.shape[1]
    slots = groups * capacity
    width = part * sides
    hidden = up_weight.shape[1]
    blocks_f = hidden // BLOCK
    lanes = -(-up_table.shape[2] // BLOCK) * BLOCK
    chunks = (1, 2)
    tall = capacity * part // BLOCK
    short = -(-capacity // 16) * 16
    vmem = pl.BlockSpec(memory_space=pltpu.VMEM)
    anywhere = pl.BlockSpec(memory_space=pl.ANY)
    trips = 3 * (groups - 1) + 6 + sum(chunks) * (groups + 2)

    def buffer(*shape):
        return pltpu.VMEM(shape, jnp.bfloat16)

    rows, turned = pl.pallas_call(
        functools.partial(layer_kernel, groups, capacity),
        out_shape=[
            jax.ShapeDtypeStruct((2, slots, part), jnp.bfloat16),
            jax.ShapeDtypeStruct((tokens.shape[0], slots), jnp.bfloat16),
        ],
        in_specs=[vmem] * 2 + [anywhere] * 5,
        out_specs=[vmem] * 2,
        scratch_shapes=[
            buffer(*up_weight.shape),
            buffer(*down_weight.shape),
            pltpu.VMEM(up_table.shape, jnp.int32),
            pltpu.VMEM(down_table.shape, jnp.int32),
            buffer(*cotangent.shape),
            buffer(blocks_f, slots, width),
            buffer(blocks_f, slots, width),
            buffer(groups, short, lanes),
            buffer(groups, tall, BLOCK),
            buffer(groups, tall, BLOCK),
            buffer(groups, short, lanes),
            buffer(sides, groups, tall, BLOCK),
            buffer(sides, groups, tall, BLOCK),
            pltpu.VMEM((slots, width), jnp.float32),
            buffer(slots, width),
            buffer(slots, width),
            buffer(slots, hidden),
            buffer(slots, hidden),
            pltpu.VMEM((slots, hidden), jnp.float32),
            *[buffer(n, sides, slots, part // n) for n in chunks],
            *[buffer(n, 2, slots, part // n) for n in chunks],
            *[buffer(n, slots, part // n) for n in chunks * 2],
            *[buffer(n, groups, tall // n, BLOCK) for n in chunks * 2],
            pltpu.SemaphoreType.DMA((5,)),
            pltpu.SemaphoreType.DMA((trips,)),
            pltpu.SemaphoreType.DMA((trips,)),
        ],
        compiler_params=pltpu.CompilerParams(
            collective_id=0, has_side_effects=True, vmem_limit_bytes=60 * 2**20
        ),
        name="layer",
    )(tokens, pair_row, cotangent, up_table, down_table, up_weight, down_weight)
    return pl.pallas_call(
        settle_kernel,
        out_shape=[jax.ShapeDtypeStruct(tokens.shape, jnp.bfloat16)] * 2,
        in_specs=[vmem] * 2,
        out_specs=[vmem] * 2,
        name="settle",
    )(rows, turned)


def place(pair_ids, groups, capacity):
    target = pair_ids % groups
    matches = (target[:, None] == jnp.arange(groups, dtype=jnp.int32)[None, :]).astype(jnp.int32)
    before = jnp.sum((jnp.cumsum(matches, axis=0) - matches) * matches, axis=1)
    position = target * capacity + before
    slots = jnp.arange(groups * capacity, dtype=jnp.int32)
    return (position[None, :] == slots[:, None]).astype(jnp.bfloat16)


def swap(values, groups, capacity):
    width = values.shape[1]
    moved = lax.all_to_all(
        values.reshape(groups, capacity, width), "dp", split_axis=0, concat_axis=0, tiled=True
    )
    return moved.reshape(groups * capacity, width)


def per_device(tokens, cotangent, pair_ids, up_mask, down_mask, up_weight, down_weight):
    groups = lax.axis_size("dp")
    tok_count, part = tokens.shape
    pairs = up_mask.shape[0]
    capacity = max(2, (3 * tok_count + 2 * groups - 1) // (2 * groups))
    slot_count = groups * capacity
    lanes = -(-pairs // BLOCK) * BLOCK
    pad = ((0, 0), (0, 0), (0, lanes - pairs))
    up_table = jnp.transpose(up_mask, (1, 2, 0))
    down_table = jnp.transpose(down_mask, (1, 2, 0))
    sides = lax.axis_size("tensor")
    if sides == 4 and part % 256 == 0 and up_weight.shape[1] % 1024 == 0 and capacity * part // 256 % 16 == 0 and capacity % 8 == 0:
        return layer(
            tokens, cotangent, pair_ids.reshape(1, tok_count), up_table, down_table, up_weight,
            down_weight[0], groups, capacity, sides,
        )

    placer = place(pair_ids, groups, capacity)
    known = (pair_ids[:, None] == jnp.arange(lanes, dtype=jnp.int32)[None, :]).astype(jnp.bfloat16)
    leaving = jnp.concatenate([tokens, cotangent, known], axis=1)
    moved = swap(dot(placer, leaving).astype(jnp.bfloat16), groups, capacity)
    both = jnp.stack([moved[:, :part], moved[:, part : 2 * part]])
    whole = lax.all_gather(both, "tensor", axis=2, tiled=True)
    mixed_part, input_part = compute(
        whole[0], whole[1], moved[:, 2 * part :], jnp.pad(up_table, pad), jnp.pad(down_table, pad), up_weight, down_weight[0]
    )
    summed = lax.psum_scatter(
        jnp.stack([mixed_part, input_part]), "tensor", scatter_dimension=2, tiled=True
    )
    back = swap(jnp.concatenate([summed[0], summed[1]], axis=1), groups, capacity)
    out = lax.dot_general(
        placer, back, (((0,), (0,)), ((), ())), preferred_element_type=jnp.float32
    ).astype(jnp.bfloat16)
    return out[:, :part], out[:, part:]


def solution(mesh):
    return jax.shard_map(
        per_device,
        mesh=mesh,
        in_specs=(
            P("dp", "tensor"),
            P("dp", "tensor"),
            P("dp"),
            P(None, None, "tensor"),
            P(None, "tensor", None),
            P(None, "tensor"),
            P("dp", "tensor", None),
        ),
        out_specs=(P("dp", "tensor"), P("dp", "tensor")),
        check_vma=False,
    )
```
